128 devices in a mesh: dp: 8 (over z, core), table: 16 (over x, y).
Axes of the slice: x: 4, y: 4, z: 4, core: 2. Of those that a mesh axis runs over, the one named last changes fastest.
Arguments:
- history_lengths: int32 [8, 32], P(None, 'table'), may hold values from 1 to 256, as said below
- balance_list: int32 [8, 32], P(None, 'table'), may hold values from 0 to 15, as said below
- owner_device: int32 [256, 256, 1], P(('dp', 'table')), may hold values from 0 to 127; in each aligned block of 512 rows (0 to 511, 512 to 1023, ..., all dimensions but the last counted through in order) at most 8 rows name the same one
- owner_row: int32 [256, 256], P(('dp', 'table')), may hold values from 0 to 4095
- width_class: int32 [524288], replicated, may hold values from 0 to 2
- slab_index: int32 [524288], P(('dp', 'table')), may hold values from 0 to 2047
- narrow_table: bfloat16 [131072, 128], P(('dp', 'table')), may hold values from -6 to 6
- middle_table: bfloat16 [262144, 128], P(('dp', 'table')), may hold values from -6 to 6
- wide_table: bfloat16 [262144, 256], P(('dp', 'table')), may hold values from -6 to 6
- narrow_lift: bfloat16 [64, 512], replicated, may hold values from -0.75 to 0.75
- middle_lift: bfloat16 [128, 512], replicated, may hold values from -0.5 to 0.5
- wide_lift: bfloat16 [256, 512], replicated, may hold values from -0.375 to 0.375
- joined_weight: bfloat16 [512, 2048], replicated, may hold values from -0.25 to 0.25
- output_weight: bfloat16 [512, 512], replicated, may hold values from -0.25 to 0.25
- cotangent: bfloat16 [256, 256, 512], P(('dp', 'table')), may hold values from -6 to 6
Outputs:
- layer_output: bfloat16 [256, 256, 512], P(('dp', 'table'))
- narrow_grad: float32 [131072, 128], P(('dp', 'table'))
- middle_grad: float32 [262144, 128], P(('dp', 'table'))
- wide_grad: float32 [262144, 256], P(('dp', 'table'))
- narrow_delta: float32 [64, 512], replicated
- middle_delta: float32 [128, 512], replicated
- wide_delta: float32 [256, 512], replicated
The draws below stay inside these ranges and needn't reach their ends.
Inputs may be any that keep to these rules, and one draw needn't show every extreme that they name: `history_lengths`: at least one history has length 256. `balance_list`: an entry j names the history in slot j mod 2 of the device with dp index j // 2 and the same table index. Each slot holds its own device's history of the same slot, except exactly 1 slot of each device, which holds a history of the device whose dp index is the own one XOR half the dp axis size; it is the slot whose own history goes to that device. For each table index the entries form a permutation. `owner_device`: among the 512 tokens of one device (aligned blocks in the order of histories and positions) at most 8 name the same owner, a bound that some block reaches.
All inputs are finite; a program needn't handle non-finite values.
Results may differ from the reference program's by a relative error of at most 0.017.
Values may be sent and summed in bfloat16 or wider, within the bound.
No kernel may reach another device: no remote copies, remote signals or barrier semaphores. Data moves between devices by JAX's collectives and lax.ppermute only.
A program may use at most 128 MiB of HBM per device.

```python
import math
import jax
import jax.numpy as jnp
import numpy as np
from jax import lax

HEADS = 4
HEAD = 128
D = 512
MAXLEN = 256
HIST_DEV = 2
MOVES = 1
BLOCK = 128
CAP = 8
ITEMS_DEV = 4096
SLAB_DEV = 2048
HISTS = 256
ITEMS = 524288
SLABS = 262144
N_DP = 8
N_TABLE = 16
DEVICES = 128


def balance_plan(key):
    first, second, third = jax.random.split(key, 3)
    grid_shape = (N_DP, N_TABLE, HIST_DEV)
    factor_one = jax.random.randint(first, grid_shape, 0, MAXLEN, dtype=jnp.int32)
    factor_two = jax.random.randint(second, grid_shape, 0, MAXLEN, dtype=jnp.int32)
    lengths_grid = 1 + factor_one * factor_two // MAXLEN
    total_hists = N_DP * N_TABLE * HIST_DEV
    chosen_one = jax.random.randint(third, (), 0, total_hists, dtype=jnp.int32)
    flat_lengths = jnp.where(jnp.arange(total_hists, dtype=jnp.int32) == chosen_one, MAXLEN, lengths_grid.reshape(total_hists))
    lengths_grid = flat_lengths.reshape(grid_shape)
    blocks = (lengths_grid + BLOCK - 1) // BLOCK
    costs = jnp.sum(blocks * blocks, axis=2)
    ranks_dp = jnp.arange(N_DP, dtype=jnp.int32)
    partner = ranks_dp ^ N_DP // 2
    heavy = (costs > costs[partner]) | (costs == costs[partner]) & (ranks_dp < partner)[:, None]
    slots_range = jnp.arange(HIST_DEV, dtype=jnp.int32)
    scores = lengths_grid * HIST_DEV + slots_range
    descending = jnp.argsort(-scores, axis=2, stable=True).astype(jnp.int32)
    ascending = jnp.argsort(scores, axis=2, stable=True).astype(jnp.int32)
    given = jnp.where(heavy[:, :, None], descending, ascending)[:, :, :MOVES]
    incoming = partner[:, None, None] * HIST_DEV + given[partner]
    base = jnp.broadcast_to(ranks_dp[:, None, None] * HIST_DEV + slots_range, grid_shape)
    struck = given[:, :, :, None] == slots_range
    landed = jnp.sum(jnp.where(struck, incoming[:, :, :, None], 0), axis=2)
    plan_grid = jnp.where(jnp.any(struck, axis=2), landed, base)
    return (lengths_grid.reshape(N_DP, N_TABLE * HIST_DEV).astype(jnp.int32), plan_grid.reshape(N_DP, N_TABLE * HIST_DEV).astype(jnp.int32))


def draw_history_lengths(key, part):
    lengths_drawn, plan_drawn = balance_plan(key)
    return lengths_drawn


def draw_balance_list(key, part):
    lengths_drawn, plan_drawn = balance_plan(key)
    return plan_drawn


def plant(array, key, low, top_value):
    place = [jax.random.randint(jax.random.fold_in(key, axis), (), 0, length) for axis, length in enumerate(array.shape)]
    longest = array.shape.index(max(array.shape))
    beside = place[:longest] + [(place[longest] + 1) % array.shape[longest]] + place[longest + 1:]
    return array.at[tuple(place)].set(low).at[tuple(beside)].set(top_value)


def block_levels(stream_key, shape, shards, low, high):
    def one(dim, blocks):
        steps = jax.random.uniform(jax.random.fold_in(jax.random.fold_in(stream_key, 6), dim), (blocks,), jnp.float32, low / len(shards), high / len(shards))
        return jnp.repeat(jnp.exp(steps), shape[dim] // blocks).reshape((-1,) + (1,) * (len(shape) - dim - 1))

    factor_of = one(*shards[0])
    for cut in shards[1:]:
        factor_of = factor_of * one(*cut)
    return factor_of


def cumulative_ranks(number_of, slope):
    loads = [(1 << 20) // math.isqrt(standing ** slope) + 1 for standing in range(1, number_of + 1)]
    deviation = 1 + sum(loads) // (1 << 30)
    return np.cumsum(np.array([max(1, weight // deviation) for weight in loads]))


def ranked(stream_key, extent, count, skew):
    listing = cumulative_ranks(count, skew)
    pick = jax.random.randint(jax.random.fold_in(stream_key, 1), extent, 0, int(listing[count - 1]))
    grade = jnp.searchsorted(jnp.asarray(listing, jnp.int32), pick, side="right")
    return jax.random.permutation(jax.random.fold_in(stream_key, 2), count)[grade].astype(jnp.int32)


def shared_out(rng, own, number, rows, count, top, reach, slope):
    order = jax.random.permutation(rng, count)
    crowded, ordinary = shares(count, rows * top, reach, slope, True), shares(count, rows * top, reach, slope, False)
    places = jnp.arange(count)

    def named(sizes, turn):
        used = int((sizes > 0).sum())
        fixed = max(1, used // 4)
        passed = fixed + (places - fixed + turn * (used - fixed)) % max(1, count - fixed)
        return jnp.zeros((count,), jnp.int32).at[order[jnp.where(places < fixed, places, passed)]].set(jnp.asarray(sizes, jnp.int32))

    sizes = jnp.where(number % 4 == 0, named(crowded, number // 4), named(ordinary, number - number // 4 - 1))
    mixed = jax.random.permutation(jax.random.fold_in(own, 3), count)
    source_of, sink = mixed[0:count // 2 * 2:2], mixed[1:count // 2 * 2:2]
    margin = jnp.minimum(sizes[source_of] - 1, reach - sizes[sink]) // 2
    margin = jnp.where((source_of == order[0]) | (sink == order[0]) | (sizes[sink] == 0), 0, jnp.maximum(margin, 0))
    passed = jax.random.randint(jax.random.fold_in(own, 4), (count // 2,), 0, 1 << 20) % (margin + 1)
    sizes = sizes.at[source_of].add(-passed).at[sink].add(passed)
    labels = jnp.searchsorted(jnp.cumsum(sizes), jnp.arange(rows * top), side="right").astype(jnp.int32)
    listing = labels.reshape(top, rows).T
    listing = listing[jax.random.permutation(jax.random.fold_in(own, 1), rows)]
    turn = jax.random.randint(jax.random.fold_in(own, 2), (rows, 1), 0, top)
    return jnp.take_along_axis(listing, (jnp.arange(top)[None, :] + turn) % top, axis=1)


def shares(number_of, total, bound, lean, full):
    loads = [(1 << 20) // math.isqrt(standing ** lean) + 1 for standing in range(1, number_of + 1)]
    largest = bound if full else min(bound, max(-(-total // number_of), total * loads[0] // sum(loads)))
    least = 1 if total - largest >= number_of - 1 else 0
    given, spare = [largest] + [least] * (number_of - 1), total - largest - least * (number_of - 1)
    while spare > 0:
        movable = [i for i in range(1, number_of) if given[i] < largest] or [i for i in range(1, number_of) if given[i] < bound]
        whole, budget = sum([loads[i] for i in movable]), spare
        for i in movable:
            addition = min(bound - given[i], max(1, budget * loads[i] // whole), spare)
            given[i] = given[i] + addition
            spare = spare - addition
    return np.array(given)


def centred(own_key, extent, scale, reach, cuts=(), kind=jnp.bfloat16):
    gain = block_levels(own_key, extent, cuts, -0.22, 0.18) if cuts else 1.0
    array = jax.random.normal(own_key, extent, jnp.float32) * scale * gain
    return jnp.minimum(jnp.maximum(array, -reach), reach).astype(kind)


def setup_inputs(seed: int = 0) -> dict:
    seeds = jax.random.split(jax.random.key(seed), 16)
    history_lengths = draw_history_lengths(jax.random.fold_in(seeds[15], 71), 0)
    balance_list = draw_balance_list(jax.random.fold_in(seeds[15], 71), 0)
    owner_device_keys = jax.random.split(jax.random.fold_in(seeds[2], 1), HISTS * MAXLEN // (HIST_DEV * MAXLEN))
    owner_device_turns = jax.random.permutation(jax.random.fold_in(seeds[2], 3), HISTS * MAXLEN // (HIST_DEV * MAXLEN))
    owner_device = jax.vmap(lambda own, number: shared_out(jax.random.fold_in(seeds[2], 2), own, number, HIST_DEV * MAXLEN, DEVICES, 1, CAP, 2))(owner_device_keys, owner_device_turns).reshape((HISTS, MAXLEN, 1))
    owner_row = plant(ranked(seeds[3], (HISTS, MAXLEN), ITEMS_DEV, 2), jax.random.fold_in(seeds[3], 3), 0, ITEMS_DEV - 1).astype(jnp.int32)
    width_class = plant(jax.random.randint(seeds[4], (ITEMS,), 0, 3), jax.random.fold_in(seeds[4], 1), 0, 2).astype(jnp.int32)
    slab_index = plant(jax.random.randint(seeds[5], (ITEMS,), 0, SLAB_DEV), jax.random.fold_in(seeds[5], 1), 0, SLAB_DEV - 1).astype(jnp.int32)
    narrow_table = centred(seeds[6], (SLABS // 2, 128), 1.0, 6.0, ((0, 128),))
    middle_table = centred(seeds[7], (SLABS, 128), 1.0, 6.0, ((0, 128),))
    wide_table = centred(seeds[8], (SLABS, 256), 1.0, 6.0, ((0, 128),))
    narrow_lift = centred(seeds[9], (64, D), 64 ** -0.5, 0.75)
    middle_lift = centred(seeds[10], (128, D), 128 ** -0.5, 0.5)
    wide_lift = centred(seeds[11], (256, D), 256 ** -0.5, 0.375)
    joined_weight = centred(seeds[12], (D, 4 * D), D ** -0.5, 0.25)
    output_weight = centred(seeds[13], (D, D), D ** -0.5, 0.25)
    cotangent = centred(seeds[14], (HISTS, MAXLEN, D), 0.5, 6.0, ((0, 128),))
    return dict(history_lengths=history_lengths, balance_list=balance_list, owner_device=owner_device, owner_row=owner_row, width_class=width_class, slab_index=slab_index, narrow_table=narrow_table, middle_table=middle_table, wide_table=wide_table, narrow_lift=narrow_lift, middle_lift=middle_lift, wide_lift=wide_lift, joined_weight=joined_weight, output_weight=output_weight, cotangent=cotangent)


def normalize(values):
    centre = values - lax.optimization_barrier(jnp.mean(values, axis=-1, keepdims=True))
    spread = lax.optimization_barrier(jnp.mean(centre * centre, axis=-1, keepdims=True))
    return centre * lax.rsqrt(spread + 1e-06)

def fetch_rows(narrow_table, middle_table, wide_table, slab_rows, classes):
    amount = slab_rows.shape[0]
    packed = narrow_table[slab_rows // 2]
    halves = jnp.where((slab_rows % 2 == 0)[:, None], packed[:, :64], packed[:, 64:])
    padded_narrow = jnp.concatenate([halves, jnp.zeros((amount, 192), halves.dtype)], axis=1)
    padded_middle = jnp.concatenate([middle_table[slab_rows], jnp.zeros((amount, 128), halves.dtype)], axis=1)
    return jnp.where((classes == 2)[:, None], wide_table[slab_rows], jnp.where((classes == 1)[:, None], padded_middle, padded_narrow))

def expand_rows(padded, classes):
    amount = padded.shape[0]
    return jnp.concatenate([jnp.where((classes == 0)[:, None], padded[:, :64], 0), jnp.where((classes == 1)[:, None], padded[:, :128], 0), jnp.where((classes == 2)[:, None], padded, 0), jnp.zeros((amount, 64), padded.dtype)], axis=1)

def band_rows(spread_grad, classes):
    amount = spread_grad.shape[0]
    narrow_part = jnp.concatenate([spread_grad[:, :64], jnp.zeros((amount, 192), jnp.float32)], axis=1)
    middle_part = jnp.concatenate([spread_grad[:, 64:192], jnp.zeros((amount, 128), jnp.float32)], axis=1)
    chosen = jnp.where((classes == 2)[:, None], spread_grad[:, 192:448], jnp.where((classes == 1)[:, None], middle_part, narrow_part))
    return chosen.astype(jnp.bfloat16)

def add_rows(narrow_sum, middle_sum, wide_sum, row_grads, slab_rows, classes):
    widened = lax.optimization_barrier(row_grads).astype(jnp.float32)
    amount = widened.shape[0]
    wide_sum = wide_sum.at[slab_rows].add(jnp.where((classes == 2)[:, None], widened, 0.0))
    middle_sum = middle_sum.at[slab_rows].add(jnp.where((classes == 1)[:, None], widened[:, :128], 0.0))
    narrow_part = jnp.where((classes == 0)[:, None], widened[:, :64], 0.0)
    blank = jnp.zeros((amount, 64), jnp.float32)
    placed = jnp.where((slab_rows % 2 == 0)[:, None], jnp.concatenate([narrow_part, blank], axis=1), jnp.concatenate([blank, narrow_part], axis=1))
    narrow_sum = narrow_sum.at[slab_rows // 2].add(placed)
    return (narrow_sum, middle_sum, wide_sum)

def layer(inputs, length, joined_weight, output_weight):
    rows_total = inputs.shape[0]
    width = inputs.shape[1]
    widened = inputs.astype(jnp.float32)
    normed = normalize(widened).astype(jnp.bfloat16)
    joined = jax.nn.silu(jnp.dot(normed, joined_weight, preferred_element_type=jnp.float32)).astype(jnp.bfloat16)
    gating = joined[:, :width]
    values_heads = joined[:, width:2 * width].reshape(rows_total, HEADS, HEAD).astype(jnp.float32)
    queries = joined[:, 2 * width:3 * width].reshape(rows_total, HEADS, HEAD).astype(jnp.float32)
    keys_heads = joined[:, 3 * width:].reshape(rows_total, HEADS, HEAD).astype(jnp.float32)
    scores = jnp.einsum('qhe,khe->hqk', queries, keys_heads)
    places = jnp.arange(rows_total, dtype=jnp.int32)
    allowed = (places[None, :] <= places[:, None]) & (places[None, :] < length)
    weights = jnp.where(allowed[None], jax.nn.silu(scores) / MAXLEN, 0.0).astype(jnp.bfloat16)
    mixed = jnp.einsum('hqk,khe->qhe', weights.astype(jnp.float32), values_heads).reshape(rows_total, width)
    gated = (normalize(mixed) * gating.astype(jnp.float32)).astype(jnp.bfloat16)
    result = jnp.dot(gated, output_weight, preferred_element_type=jnp.float32) + widened
    return jnp.where((places < length)[:, None], result, 0.0).astype(jnp.bfloat16)

def reference(history_lengths, balance_list, owner_device, owner_row, width_class, slab_index, narrow_table, middle_table, wide_table, narrow_lift, middle_lift, wide_lift, joined_weight, output_weight, cotangent):
    width = narrow_lift.shape[1]
    lift_all = jnp.concatenate([narrow_lift, middle_lift, wide_lift, jnp.zeros((64, width), narrow_lift.dtype)], axis=0)

    def one_history(totals, target):
        narrow_sum, middle_sum, wide_sum, lift_sum = totals
        device = target // HIST_DEV
        data_rank = device // N_TABLE
        table_rank = device % N_TABLE
        slot_index = target % HIST_DEV
        column = table_rank * HIST_DEV
        source = balance_list[data_rank, column + slot_index]
        source_rank = source // HIST_DEV
        source_slot = source % HIST_DEV
        anchor = (source_rank * N_TABLE + table_rank) * HIST_DEV + source_slot
        length = history_lengths[source_rank, column + source_slot]
        owners = owner_device[anchor, :, 0]
        item_ids = owners * ITEMS_DEV + owner_row[anchor]
        classes = width_class[item_ids]
        slab_rows = owners * SLAB_DEV + slab_index[item_ids]
        spread = expand_rows(fetch_rows(narrow_table, middle_table, wide_table, slab_rows, classes), classes)
        embedded = jnp.dot(spread, lift_all, preferred_element_type=jnp.float32).astype(jnp.bfloat16)
        output, pullback = jax.vjp(lambda inputs: layer(inputs, length, joined_weight, output_weight), embedded)
        embed_grad, = pullback(cotangent[target])
        spread_grad = lax.dot_general(embed_grad, lift_all, (((1,), (1,)), ((), ())), preferred_element_type=jnp.float32)
        row_grads = band_rows(spread_grad, classes)
        narrow_sum, middle_sum, wide_sum = add_rows(narrow_sum, middle_sum, wide_sum, row_grads, slab_rows, classes)
        lift_sum = lift_sum + jnp.dot(spread.T, embed_grad, preferred_element_type=jnp.float32)
        return ((narrow_sum, middle_sum, wide_sum, lift_sum), output)
    start = (jnp.zeros((SLABS // 2, 128), jnp.float32), jnp.zeros((SLABS, 128), jnp.float32), jnp.zeros((SLABS, 256), jnp.float32), jnp.zeros((512, width), jnp.float32))
    totals, outputs = lax.scan(one_history, start, jnp.arange(HISTS, dtype=jnp.int32))
    narrow_sum, middle_sum, wide_sum, lift_sum = totals
    return (outputs, narrow_sum, middle_sum, wide_sum, lift_sum[:64], lift_sum[64:192], lift_sum[192:448])
```

```python
import jax
import jax.numpy as jnp
from jax import lax
from jax.experimental import pallas as pl
from jax.experimental.pallas import tpu as pltpu
from jax.sharding import PartitionSpec as P

HEADS = 4
HEAD = 128
MAXLEN = 256
WIDTH = 512
CAP = 8
LANES = 128

F32 = jnp.float32
BF16 = jnp.bfloat16
I32 = jnp.int32


def iota(shape, dim):
    return lax.broadcasted_iota(I32, shape, dim)


def one_hot(mask):
    return jnp.where(mask, 1.0, 0.0).astype(BF16)


def dot(a, b):
    return jnp.dot(a, b, preferred_element_type=F32)


def dot_nt(a, b):
    return lax.dot_general(a, b, (((1,), (1,)), ((), ())), preferred_element_type=F32)


def dot_tn(a, b):
    return lax.dot_general(a, b, (((0,), (0,)), ((), ())), preferred_element_type=F32)


def to_column(row):
    eye = iota((LANES, LANES), 0) == iota((LANES, LANES), 1)
    parts = []
    for start in range(0, row.shape[1], LANES):
        piece = row[:, start : start + LANES].astype(F32)
        parts.append(jnp.sum(jnp.where(eye, piece, 0.0), axis=1, keepdims=True))
    return jnp.concatenate(parts, axis=0).astype(I32)


def to_row(column):
    eye = iota((LANES, LANES), 0) == iota((LANES, LANES), 1)
    parts = []
    for start in range(0, column.shape[0], LANES):
        piece = column[start : start + LANES].astype(F32)
        parts.append(jnp.sum(jnp.where(eye, piece, 0.0), axis=0, keepdims=True))
    return jnp.concatenate(parts, axis=1).astype(I32)


def lane_sum(mask, values):
    return jnp.sum(jnp.where(mask, values, 0.0), axis=1, keepdims=True).astype(I32)


def flat_row(ref):
    return jnp.concatenate([ref[0:1, :], ref[1:2, :]], axis=1)


def request_kernel(owner_ref, item_ref, request_ref, slot_ref):
    devices = request_ref.shape[0]
    owner = flat_row(owner_ref)
    item = flat_row(item_ref)
    tokens = owner.shape[1]
    named = iota((devices, tokens), 0) == owner
    hot = one_hot(named)
    earlier = one_hot(iota((tokens, tokens), 0) < iota((tokens, tokens), 1))
    before = dot(hot, earlier)
    rank = jnp.sum(jnp.where(named, before, 0.0), axis=0, keepdims=True).astype(I32)
    place = iota((2 * CAP, tokens), 0)
    value = jnp.where(place < CAP, item >> 6, item & 63)
    table = jnp.where((place & (CAP - 1)) == rank, value, 0).astype(F32).astype(BF16)
    filled = dot_nt(hot, table).astype(I32)
    request_ref[...] = filled[:, :CAP] * 64 + filled[:, CAP:]
    slot = owner * CAP + rank
    half = tokens // 2
    slot_ref[0:1, :] = slot[:, :half]
    slot_ref[1:2, :] = slot[:, half:]


def class_kernel(owner_ref, item_ref, class_list_ref, class_ref):
    item = to_column(flat_row(item_ref))
    line = to_column(flat_row(owner_ref)) * (4096 // LANES) + (item >> 7)
    tokens = line.shape[0]
    lines = class_list_ref.shape[0]
    step = 512
    total = jnp.zeros((tokens, LANES), F32)
    for start in range(0, lines, step):
        hot = one_hot(iota((tokens, step), 1) + start == line)
        total += dot(hot, class_list_ref[start : start + step, :].astype(F32).astype(BF16))
    class_ref[...] = lane_sum(iota((tokens, LANES), 1) == (item & 127), total)


def owner_kernel(asked_ref, class_ref, slab_ref, narrow_ref, middle_ref, wide_ref, reply_ref, code_ref):
    asked = asked_ref[...]
    sources = asked.shape[0]
    amount = sources * CAP
    expand = one_hot((iota((amount, sources), 0) >> 3) == iota((amount, sources), 1))
    mine = (iota((amount, CAP), 0) & (CAP - 1)) == iota((amount, CAP), 1)
    high = lane_sum(mine, dot(expand, (asked >> 7).astype(F32).astype(BF16)))
    low = lane_sum(mine, dot(expand, (asked & 127).astype(F32).astype(BF16)))
    groups = slab_ref.shape[0]
    slab_list = slab_ref[...]
    marks = jnp.concatenate([slab_list & 127, (slab_list >> 7) + 16 * class_ref[...]], axis=1)
    found = dot(one_hot(iota((amount, groups), 1) == high), marks.astype(F32).astype(BF16))
    mine = iota((amount, LANES), 1) == low
    code_low = lane_sum(mine, found[:, :LANES])
    code_high = lane_sum(mine, found[:, LANES:])
    code_ref[...] = code_high * LANES + code_low
    step = 256
    lines = wide_ref.shape[0]
    packed_lines = narrow_ref.shape[0]

    @pl.loop(0, amount // step)
    def _(block):
        rows = pl.ds(pl.multiple_of(block * step, step), step)
        code = code_ref[rows, :]
        kind = code >> 11
        slab = code & 2047
        hot = one_hot(iota((step, lines), 1) == jnp.where(kind == 0, slab >> 1, slab))
        from_wide = dot(hot, wide_ref[...])
        from_middle = dot(hot, middle_ref[...])
        from_narrow = dot(hot[:, :packed_lines], narrow_ref[...])
        from_narrow = jnp.where((slab & 1) == 1, pltpu.roll(from_narrow, 64, 1), from_narrow)
        from_narrow = jnp.where(iota((step, LANES), 1) < 64, from_narrow, 0.0)
        left = jnp.where(kind == 2, from_wide[:, :LANES], jnp.where(kind == 1, from_middle, from_narrow))
        right = jnp.where(kind == 2, from_wide[:, LANES:], 0.0)
        reply_ref[rows, :] = jnp.concatenate([left, right], axis=1).astype(BF16)


def foreign_slot(rank_ref, list_ref):
    rank = rank_ref[0]
    return jnp.where((list_ref[rank, 0] >> 1) != rank, 0, 1)


def pick_rows(slot_ref, which, landed_ref):
    slot = to_column(slot_ref[pl.ds(which, 1), :])
    hot = one_hot(iota((slot.shape[0], landed_ref.shape[0]), 1) == slot)
    return dot(hot, landed_ref[...]).astype(BF16)


def give_kernel(rank_ref, list_ref, slot_ref, landed_ref, class_ref, given_ref):
    which = foreign_slot(rank_ref, list_ref)
    rows = given_ref.shape[0]
    given_ref[:, :256] = pick_rows(slot_ref, which, landed_ref)
    kind = class_ref[pl.ds(pl.multiple_of(which * rows, rows), rows), :]
    given_ref[:, 256:] = jnp.broadcast_to(kind.astype(F32).astype(BF16), (rows, LANES))


def mean(values):
    return jnp.sum(values, axis=1, keepdims=True) * (1.0 / WIDTH)


def normalize(values):
    centre = values - mean(values)
    scale = lax.rsqrt(mean(centre * centre) + 1e-06)
    return centre * scale, scale


def normalize_grad(grad, normed, scale):
    return scale * (grad - mean(grad) - normed * mean(grad * normed))


def sigmoid(values):
    return 0.5 * jnp.tanh(0.5 * values) + 0.5


def rounded(values):
    return values.astype(BF16).astype(F32)


def layer(raw, kind, length, cotangent, lift_ref, joined_weight_ref, output_weight_ref, slope_ref, curve_ref):
    rows = raw.shape[0]
    zero = jnp.zeros((), BF16)
    spread = jnp.concatenate(
        [
            jnp.where(kind == 2, raw, zero),
            jnp.where(kind == 1, raw[:, :LANES], zero),
            jnp.where(kind == 0, raw[:, :LANES], zero),
        ],
        axis=1,
    )
    widened = rounded(dot(spread, lift_ref[...]))
    normed, scale = normalize(widened)
    normed_low = normed.astype(BF16)
    joined = []
    for part in range(4):
        columns = slice(part * WIDTH, (part + 1) * WIDTH)
        before = dot(normed_low, joined_weight_ref[:, columns])
        gate = sigmoid(before)
        joined.append((before * gate).astype(BF16))
        slope_ref[:, columns] = gate * (1.0 + before * (1.0 - gate))
    gating, values, queries, keys = joined
    gating = gating.astype(F32)
    across = iota((rows, rows), 1)
    allowed = (across <= iota((rows, rows), 0)) & (across < length)
    factor = jnp.where(allowed, 1.0 / MAXLEN, 0.0)
    weights = []
    mixed = []
    for head in range(HEADS):
        columns = slice(head * HEAD, (head + 1) * HEAD)
        scores = dot_nt(queries[:, columns], keys[:, columns])
        gate = sigmoid(scores)
        scaled = gate * factor
        weights.append((scores * scaled).astype(BF16))
        curve_ref[head] = scaled * (1.0 + scores * (1.0 - gate))
        mixed.append(dot(weights[head], values[:, columns]))
    mixed_normed, mixed_scale = normalize(jnp.concatenate(mixed, axis=1))
    gated = (mixed_normed * gating).astype(BF16)
    result = dot(gated, output_weight_ref[...]) + widened
    valid = iota((rows, 1), 0) < length
    output = jnp.where(valid, result, 0.0).astype(BF16)

    result_grad = jnp.where(valid, cotangent, zero)
    gated_grad = rounded(dot_nt(result_grad, output_weight_ref[...]))
    gating_grad = (gated_grad * mixed_normed).astype(BF16)
    mixed_grad = normalize_grad(gated_grad * gating, mixed_normed, mixed_scale).astype(BF16)
    values_grad = []
    queries_grad = []
    keys_grad = []
    for head in range(HEADS):
        columns = slice(head * HEAD, (head + 1) * HEAD)
        own = mixed_grad[:, columns]
        weights_grad = rounded(dot_nt(own, values[:, columns]))
        scores_grad = (weights_grad * curve_ref[head]).astype(BF16)
        values_grad.append(dot_tn(weights[head], own).astype(BF16))
        queries_grad.append(dot(scores_grad, keys[:, columns]).astype(BF16))
        keys_grad.append(dot_tn(scores_grad, queries[:, columns]).astype(BF16))
    joined_grad = [gating_grad] + [jnp.concatenate(g, axis=1) for g in (values_grad, queries_grad, keys_grad)]
    normed_grad = jnp.zeros((rows, WIDTH), F32)
    for part in range(4):
        columns = slice(part * WIDTH, (part + 1) * WIDTH)
        before_grad = (joined_grad[part].astype(F32) * slope_ref[:, columns]).astype(BF16)
        normed_grad += dot_nt(before_grad, joined_weight_ref[:, columns])
    grad = normalize_grad(rounded(normed_grad), normed, scale) + result_grad.astype(F32)
    grad = grad.astype(BF16)
    spread_grad = dot_nt(grad, lift_ref[...])
    narrow_part = jnp.where(iota((rows, LANES), 1) < 64, spread_grad[:, 384:], 0.0)
    left = jnp.where(
        kind == 2, spread_grad[:, :LANES], jnp.where(kind == 1, spread_grad[:, 256:384], narrow_part)
    )
    right = jnp.where(kind == 2, spread_grad[:, LANES:256], 0.0)
    row_grad = jnp.concatenate([left, right], axis=1).astype(BF16)
    return output, row_grad, dot_tn(spread, grad)


def kept_kernel(
    rank_ref, list_ref, length_ref, slot_ref, landed_ref, class_ref, cotangent_ref, lift_ref,
    joined_weight_ref, output_weight_ref, output_ref, grad_ref, term_ref, slope_ref, curve_ref,
):
    rank = rank_ref[0]
    which = 1 - foreign_slot(rank_ref, list_ref)
    rows = grad_ref.shape[0]
    raw = pick_rows(slot_ref, which, landed_ref)
    kind = class_ref[pl.ds(pl.multiple_of(which * rows, rows), rows), :]
    output, row_grad, term = layer(
        raw, kind, length_ref[rank, which], cotangent_ref[which], lift_ref,
        joined_weight_ref, output_weight_ref, slope_ref, curve_ref,
    )
    output_ref[...] = output
    grad_ref[...] = row_grad
    term_ref[...] = term


def foreign_kernel(
    rank_ref, list_ref, length_ref, arrived_ref, cotangent_ref, lift_ref, joined_weight_ref,
    output_weight_ref, kept_output_ref, kept_term_ref, output_ref, grad_ref, term_ref, slope_ref, curve_ref,
):
    rank = rank_ref[0]
    which = foreign_slot(rank_ref, list_ref)
    source = list_ref[rank, which]
    kind = arrived_ref[:, 256:257].astype(F32).astype(I32)
    output, row_grad, term = layer(
        arrived_ref[:, :256], kind, length_ref[source >> 1, source & 1], cotangent_ref[which], lift_ref,
        joined_weight_ref, output_weight_ref, slope_ref, curve_ref,
    )
    output_ref[which] = output
    output_ref[1 - which] = kept_output_ref[...]
    grad_ref[...] = row_grad
    term_ref[...] = (term + kept_term_ref[...]).astype(BF16)


def send_kernel(rank_ref, list_ref, slot_ref, kept_grad_ref, returned_ref, term_ref, payload_ref):
    which = foreign_slot(rank_ref, list_ref)
    devices = payload_ref.shape[0]
    rows = kept_grad_ref.shape[0]
    places = iota((devices * CAP, rows), 0)
    total = dot(one_hot(places == slot_ref[pl.ds(1 - which, 1), :]), kept_grad_ref[...])
    total += dot(one_hot(places == slot_ref[pl.ds(which, 1), :]), returned_ref[...])
    term = term_ref[...].astype(F32).reshape(devices // 2, CAP, WIDTH)
    term = jnp.stack([term[:, :, :256], term[:, :, 256:]], axis=1).reshape(devices, CAP, 256)
    total = total.reshape(devices, CAP, 256)
    payload_ref[...] = jnp.concatenate([total, term], axis=1).astype(BF16)


def sum_kernel(landed_ref, share_ref):
    total = jnp.sum(landed_ref[...].astype(F32), axis=0)[CAP:]
    share_ref[...] = jnp.broadcast_to(total[None].astype(BF16), share_ref.shape)


def scatter_kernel(landed_ref, code_ref, narrow_ref, middle_ref, wide_ref):
    sources = landed_ref.shape[0]
    amount = sources * CAP
    grads = landed_ref[...].astype(F32)[:, :CAP, :].reshape(amount, 256)
    code = code_ref[...]
    kind = code >> 11
    slab = code & 2047
    line = to_row(jnp.where(kind == 0, slab >> 1, slab))
    wide = jnp.where(kind == 2, grads, 0.0).astype(BF16)
    middle = jnp.where(kind == 1, grads[:, :LANES], 0.0).astype(BF16)
    narrow = jnp.where((kind == 0) & (iota((amount, LANES), 1) < 64), grads[:, :LANES], 0.0)
    narrow = jnp.where((slab & 1) == 1, pltpu.roll(narrow, 64, 1), narrow).astype(BF16)
    step = 256
    for start in range(0, wide_ref.shape[0], step):
        hot = one_hot(iota((step, amount), 0) + start == line)
        wide_ref[start : start + step, :] = dot(hot, wide)
        middle_ref[start : start + step, :] = dot(hot, middle)
        if start < narrow_ref.shape[0]:
            narrow_ref[start : start + step, :] = dot(hot, narrow)


def delta_kernel(shares_ref, narrow_ref, middle_ref, wide_ref):
    devices = shares_ref.shape[0]
    shares = shares_ref[...].astype(F32).reshape(devices // 2, 2, CAP, 256)
    for half in range(2):
        columns = slice(half * 256, (half + 1) * 256)
        whole = shares[:, half].reshape(devices // 2 * CAP, 256)
        wide_ref[:, columns] = whole[:256]
        middle_ref[:, columns] = whole[256:384]
        narrow_ref[:, columns] = whole[384:448]


def call(kernel, outs, args, smem=0, scratch=(), flops=0, limit=32):
    specs = [pl.BlockSpec(memory_space=pltpu.SMEM)] * smem
    specs += [pl.BlockSpec(memory_space=pltpu.VMEM)] * (len(args) - smem)
    shapes = [jax.ShapeDtypeStruct(shape, dtype) for shape, dtype in outs]
    moved = sum(a.size * a.dtype.itemsize for a in args) + sum(s.size * s.dtype.itemsize for s in shapes)
    return pl.pallas_call(
        kernel,
        out_shape=shapes,
        in_specs=specs,
        out_specs=[pl.BlockSpec(memory_space=pltpu.VMEM)] * len(shapes),
        scratch_shapes=list(scratch),
        cost_estimate=pl.CostEstimate(flops=flops, bytes_accessed=moved, transcendentals=0),
        compiler_params=pltpu.CompilerParams(vmem_limit_bytes=limit << 20),
    )(*args)


def exchange(array):
    return lax.all_to_all(array, ("dp", "table"), split_axis=0, concat_axis=0, tiled=True)


def body(
    history_lengths,
    balance_list,
    owner_device,
    owner_row,
    width_class,
    slab_index,
    narrow_table,
    middle_table,
    wide_table,
    narrow_lift,
    middle_lift,
    wide_lift,
    joined_weight,
    output_weight,
    cotangent,
):
    data_size = lax.axis_size("dp")
    table_size = lax.axis_size("table")
    devices = data_size * table_size
    rows = cotangent.shape[1]
    items = slab_index.shape[0]
    amount = devices * CAP
    data_rank = lax.axis_index("dp")
    self_rank = data_rank * table_size + lax.axis_index("table")
    rank = data_rank.reshape(1).astype(I32)
    owner = owner_device.reshape(owner_row.shape)
    class_list = width_class.reshape(-1, LANES)
    partners = [(i, i ^ (data_size // 2)) for i in range(data_size)]

    requests, slots = call(
        request_kernel, [((devices, CAP), I32), (owner.shape, I32)], (owner, owner_row), flops=10**8
    )
    asked = exchange(requests)
    (kinds,) = call(
        class_kernel, [((2 * rows, 1), I32)], (owner, owner_row, class_list), flops=10**9
    )
    own_classes = lax.dynamic_slice(class_list, (self_rank * (items // LANES), 0), (items // LANES, LANES))
    lift_all = jnp.concatenate(
        [wide_lift, middle_lift, narrow_lift, jnp.zeros((64, WIDTH), BF16)], axis=0
    )
    replies, codes = call(
        owner_kernel,
        [((amount, 256), BF16), ((amount, 1), I32)],
        (asked, own_classes, slab_index.reshape(-1, LANES), narrow_table, middle_table, wide_table),
        flops=3 * 10**9,
    )
    landed = exchange(replies)
    (given,) = call(
        give_kernel, [((rows, 384), BF16)], (rank, balance_list, slots, landed, kinds), smem=2, flops=10**8
    )
    arrived = lax.ppermute(given, "dp", partners)
    scratch = (pltpu.VMEM((rows, 4 * WIDTH), F32), pltpu.VMEM((HEADS, rows, rows), F32))
    kept_output, kept_grad, kept_term = call(
        kept_kernel,
        [((rows, WIDTH), BF16), ((rows, 256), BF16), ((WIDTH, WIDTH), F32)],
        (rank, balance_list, history_lengths, slots, landed, kinds, cotangent, lift_all, joined_weight, output_weight),
        smem=3,
        scratch=scratch,
        flops=5 * 10**9,
    )
    output, foreign_grad, term = call(
        foreign_kernel,
        [(cotangent.shape, BF16), ((rows, 256), BF16), ((WIDTH, WIDTH), BF16)],
        (
            rank, balance_list, history_lengths, arrived, cotangent, lift_all, joined_weight, output_weight,
            kept_output, kept_term,
        ),
        smem=3,
        scratch=scratch,
        flops=5 * 10**9,
    )
    returned = lax.ppermute(foreign_grad, "dp", partners)
    (payload,) = call(
        send_kernel,
        [((devices, 2 * CAP, 256), BF16)],
        (rank, balance_list, slots, kept_grad, returned, term),
        smem=2,
        flops=10**9,
    )
    home = exchange(payload)
    (share,) = call(sum_kernel, [((devices, CAP, 256), BF16)], (home,))
    shares = exchange(share)
    narrow_grad, middle_grad, wide_grad = call(
        scatter_kernel,
        [(narrow_table.shape, F32), (middle_table.shape, F32), (wide_table.shape, F32)],
        (home, codes),
        flops=3 * 10**9,
    )
    narrow_delta, middle_delta, wide_delta = call(
        delta_kernel,
        [(narrow_lift.shape, F32), (middle_lift.shape, F32), (wide_lift.shape, F32)],
        (shares,),
    )
    return (output, narrow_grad, middle_grad, wide_grad, narrow_delta, middle_delta, wide_delta)


def solution(mesh):
    in_specs = (
        P(None, "table"),
        P(None, "table"),
        P(("dp", "table"), None, None),
        P(("dp", "table"), None),
        P(),
        P(("dp", "table")),
        P(("dp", "table"), None),
        P(("dp", "table"), None),
        P(("dp", "table"), None),
        P(),
        P(),
        P(),
        P(),
        P(),
        P(("dp", "table"), None, None),
    )
    out_specs = (
        P(("dp", "table"), None, None),
        P(("dp", "table"), None),
        P(("dp", "table"), None),
        P(("dp", "table"), None),
        P(),
        P(),
        P(),
    )
    return jax.shard_map(body, mesh=mesh, in_specs=in_specs, out_specs=out_specs, check_vma=False)
```

```python
import jax
import jax.numpy as jnp
from jax import lax
from jax.experimental import pallas as pl
from jax.experimental.pallas import tpu as pltpu
from jax.sharding import PartitionSpec as P

HEADS = 4
HEAD = 128
MAXLEN = 256
WIDTH = 512
CAP = 8
LANES = 128

F32 = jnp.float32
BF16 = jnp.bfloat16
I32 = jnp.int32


def iota(shape, dim):
    return lax.broadcasted_iota(I32, shape, dim)


def one_hot(mask):
    return jnp.where(mask, 1.0, 0.0).astype(BF16)


def dot(a, b):
    return jnp.dot(a, b, preferred_element_type=F32)


def dot_nt(a, b):
    return lax.dot_general(a, b, (((1,), (1,)), ((), ())), preferred_element_type=F32)


def dot_tn(a, b):
    return lax.dot_general(a, b, (((0,), (0,)), ((), ())), preferred_element_type=F32)


def to_column(row):
    eye = iota((LANES, LANES), 0) == iota((LANES, LANES), 1)
    parts = []
    for start in range(0, row.shape[1], LANES):
        piece = row[:, start : start + LANES].astype(F32)
        parts.append(jnp.sum(jnp.where(eye, piece, 0.0), axis=1, keepdims=True))
    return jnp.concatenate(parts, axis=0).astype(I32)


def to_row(column):
    eye = iota((LANES, LANES), 0) == iota((LANES, LANES), 1)
    parts = []
    for start in range(0, column.shape[0], LANES):
        piece = column[start : start + LANES].astype(F32)
        parts.append(jnp.sum(jnp.where(eye, piece, 0.0), axis=0, keepdims=True))
    return jnp.concatenate(parts, axis=1).astype(I32)


def lane_sum(mask, values):
    return jnp.sum(jnp.where(mask, values, 0.0), axis=1, keepdims=True).astype(I32)


def flat_row(ref):
    return jnp.concatenate([ref[0:1, :], ref[1:2, :]], axis=1)


def request_kernel(owner_ref, item_ref, request_ref, slot_ref):
    devices = request_ref.shape[0]
    owner = jnp.concatenate([owner_ref[0], owner_ref[1]], axis=1)
    item = flat_row(item_ref)
    tokens = owner.shape[1]
    named = iota((devices, tokens), 0) == owner
    hot = one_hot(named)
    earlier = one_hot(iota((tokens, tokens), 0) < iota((tokens, tokens), 1))
    before = dot(hot, earlier)
    rank = jnp.sum(jnp.where(named, before, 0.0), axis=0, keepdims=True).astype(I32)
    place = iota((2 * CAP, tokens), 0)
    value = jnp.where(place < CAP, item >> 6, item & 63)
    table = jnp.where((place & (CAP - 1)) == rank, value, 0).astype(F32).astype(BF16)
    filled = dot_nt(hot, table).astype(I32)
    request_ref[...] = filled[:, :CAP] * 64 + filled[:, CAP:]
    slot = owner * CAP + rank
    half = tokens // 2
    slot_ref[0:1, :] = slot[:, :half]
    slot_ref[1:2, :] = slot[:, half:]


def class_kernel(owner_ref, item_ref, class_list_ref, class_ref):
    item = to_column(flat_row(item_ref))
    owner = jnp.concatenate([owner_ref[0], owner_ref[1]], axis=1)
    line = to_column(owner) * (4096 // LANES) + (item >> 7)
    tokens = line.shape[0]
    lines = class_list_ref.shape[0]
    step = 512
    total = jnp.zeros((tokens, LANES), F32)
    for start in range(0, lines, step):
        hot = one_hot(iota((tokens, step), 1) + start == line)
        total += dot(hot, class_list_ref[start : start + step, :].astype(F32).astype(BF16))
    class_ref[...] = lane_sum(iota((tokens, LANES), 1) == (item & 127), total)


def owner_kernel(
    asked_ref, class_ref, slab_ref, narrow_ref, middle_ref, wide_ref, reply_ref, code_ref,
    narrow_here, middle_here, wide_here, copied,
):
    copies = [
        pltpu.make_async_copy(there, here, copied.at[k])
        for k, (there, here) in enumerate(
            [(wide_ref, wide_here), (middle_ref, middle_here), (narrow_ref, narrow_here)]
        )
    ]
    for copy in copies:
        copy.start()
    asked = asked_ref[...]
    sources = asked.shape[0]
    amount = sources * CAP
    expand = one_hot((iota((amount, sources), 0) >> 3) == iota((amount, sources), 1))
    mine = (iota((amount, CAP), 0) & (CAP - 1)) == iota((amount, CAP), 1)
    high = lane_sum(mine, dot(expand, (asked >> 7).astype(F32).astype(BF16)))
    low = lane_sum(mine, dot(expand, (asked & 127).astype(F32).astype(BF16)))
    groups = slab_ref.shape[0]
    slab_list = slab_ref[...]
    marks = jnp.concatenate([slab_list & 127, (slab_list >> 7) + 16 * class_ref[...]], axis=1)
    found = dot(one_hot(iota((amount, groups), 1) == high), marks.astype(F32).astype(BF16))
    mine = iota((amount, LANES), 1) == low
    code_low = lane_sum(mine, found[:, :LANES])
    code_high = lane_sum(mine, found[:, LANES:])
    code = code_high * LANES + code_low
    code_ref[...] = code
    kind = code >> 11
    slab = code & 2047
    line = jnp.where(kind == 0, slab >> 1, slab)
    for copy in copies:
        copy.wait()
    step = 256
    lines = wide_ref.shape[0]
    packed_lines = narrow_ref.shape[0]
    for start in range(0, amount, step):
        rows = slice(start, start + step)
        hot = one_hot(iota((step, lines), 1) == line[rows])
        from_wide = dot(hot, wide_here[...])
        from_middle = dot(hot, middle_here[...])
        from_narrow = dot(hot[:, :packed_lines], narrow_here[...])
        from_narrow = jnp.where((slab[rows] & 1) == 1, pltpu.roll(from_narrow, 64, 1), from_narrow)
        from_narrow = jnp.where(iota((step, LANES), 1) < 64, from_narrow, 0.0)
        here = kind[rows]
        left = jnp.where(here == 2, from_wide[:, :LANES], jnp.where(here == 1, from_middle, from_narrow))
        right = jnp.where(here == 2, from_wide[:, LANES:], 0.0)
        reply_ref[rows, :] = jnp.concatenate([left, right], axis=1).astype(BF16)


def traded_slot(rank_ref, list_ref):
    rank = rank_ref[0]
    return jnp.where((list_ref[0, rank] >> 1) != rank, 0, 1)


def give_kernel(rank_ref, list_ref, cotangent_ref, given_ref, copied):
    copy = pltpu.make_async_copy(cotangent_ref.at[traded_slot(rank_ref, list_ref)], given_ref, copied)
    copy.start()
    copy.wait()


def mean(values):
    return jnp.sum(values, axis=1, keepdims=True) * (1.0 / WIDTH)


def normalize(values):
    centre = values - mean(values)
    scale = lax.rsqrt(mean(centre * centre) + 1e-06)
    return centre * scale, scale


def normalize_grad(grad, normed, scale):
    return scale * (grad - mean(grad) - normed * mean(grad * normed))


def sigmoid(values):
    return 0.5 * jnp.tanh(0.5 * values) + 0.5


def rounded(values):
    return values.astype(BF16).astype(F32)


def layer_kernel(
    rank_ref, list_ref, length_ref, slot_ref, landed_ref, class_ref, cotangent_ref, arrived_ref,
    narrow_lift_ref, middle_lift_ref, wide_lift_ref, joined_weight_ref, output_weight_ref,
    kept_ref, given_ref, payload_ref,
    lift_here, joined_here, output_here, cotangent_here, slope_ref, curve_ref, copied,
):
    rank = rank_ref[0]
    traded = traded_slot(rank_ref, list_ref)
    kept = 1 - traded
    moves = [
        (wide_lift_ref, lift_here.at[0:256]),
        (middle_lift_ref, lift_here.at[256:384]),
        (narrow_lift_ref, lift_here.at[384:448]),
        (joined_weight_ref, joined_here),
        (output_weight_ref, output_here),
        (cotangent_ref.at[kept], cotangent_here.at[kept]),
        (arrived_ref, cotangent_here.at[traded]),
    ]
    copies = [pltpu.make_async_copy(there, here, copied.at[k]) for k, (there, here) in enumerate(moves)]
    for copy in copies:
        copy.start()
    lift_here[448:, :] = jnp.zeros((64, WIDTH), BF16)
    zero = jnp.zeros((), BF16)
    rows = kept_ref.shape[0]
    hists = slot_ref.shape[0]
    tokens = hists * rows
    devices = payload_ref.shape[0]
    amount = devices * CAP
    slot = flat_row(slot_ref)
    raw = dot(one_hot(iota((tokens, amount), 1) == to_column(slot)), landed_ref[...]).astype(BF16)
    kind = class_ref[...]
    spread = jnp.concatenate(
        [
            jnp.where(kind == 2, raw, zero),
            jnp.where(kind == 1, raw[:, :LANES], zero),
            jnp.where(kind == 0, raw[:, :LANES], zero),
        ],
        axis=1,
    )
    for copy in copies[:3]:
        copy.wait()
    widened = rounded(dot(spread, lift_here[...]))
    normed, scale = normalize(widened)
    normed_low = normed.astype(BF16)
    copies[3].wait()
    joined = []
    for part in range(4):
        columns = slice(part * WIDTH, (part + 1) * WIDTH)
        before = dot(normed_low, joined_here[:, columns])
        gate = sigmoid(before)
        joined.append((before * gate).astype(BF16))
        slope_ref[:, columns] = gate * (1.0 + before * (1.0 - gate))
    gating, values, queries, keys = joined
    gating = gating.astype(F32)
    place = iota((tokens, 1), 0)
    lengths = [length_ref[hist, rank] for hist in range(hists)]
    valid = place < jnp.where(place < rows, lengths[0], rows + lengths[1])
    across = iota((rows, rows), 1)
    causal = across <= iota((rows, rows), 0)
    weights = {}
    mixed = []
    for hist in range(hists):
        lines = slice(hist * rows, (hist + 1) * rows)
        factor = jnp.where(causal & (across < lengths[hist]), 1.0 / MAXLEN, 0.0)
        heads = []
        for head in range(HEADS):
            columns = slice(head * HEAD, (head + 1) * HEAD)
            scores = dot_nt(queries[lines, columns], keys[lines, columns])
            gate = sigmoid(scores)
            scaled = gate * factor
            weights[hist, head] = (scores * scaled).astype(BF16)
            curve_ref[hist, head] = scaled * (1.0 + scores * (1.0 - gate))
            heads.append(dot(weights[hist, head], values[lines, columns]))
        mixed.append(jnp.concatenate(heads, axis=1))
    mixed_normed, mixed_scale = normalize(jnp.concatenate(mixed, axis=0))
    gated = (mixed_normed * gating).astype(BF16)
    for copy in copies[4:]:
        copy.wait()
    result = dot(gated, output_here[...]) + widened
    output = jnp.where(valid, result, 0.0).astype(BF16)
    kept_ref[...] = jnp.where(traded == 0, output[rows:], output[:rows])
    given_ref[...] = jnp.where(traded == 0, output[:rows], output[rows:])

    cotangent = jnp.concatenate([cotangent_here[0], cotangent_here[1]], axis=0)
    result_grad = jnp.where(valid, cotangent, zero)
    gated_grad = rounded(dot_nt(result_grad, output_here[...]))
    gating_grad = (gated_grad * mixed_normed).astype(BF16)
    mixed_grad = normalize_grad(gated_grad * gating, mixed_normed, mixed_scale).astype(BF16)
    grads = [[], [], []]
    for hist in range(hists):
        lines = slice(hist * rows, (hist + 1) * rows)
        heads = [[], [], []]
        for head in range(HEADS):
            columns = slice(head * HEAD, (head + 1) * HEAD)
            own = mixed_grad[lines, columns]
            weights_grad = rounded(dot_nt(own, values[lines, columns]))
            scores_grad = (weights_grad * curve_ref[hist, head]).astype(BF16)
            heads[0].append(dot_tn(weights[hist, head], own))
            heads[1].append(dot(scores_grad, keys[lines, columns]))
            heads[2].append(dot_tn(scores_grad, queries[lines, columns]))
        for part in range(3):
            grads[part].append(jnp.concatenate(heads[part], axis=1).astype(BF16))
    joined_grad = [gating_grad] + [jnp.concatenate(g, axis=0) for g in grads]
    normed_grad = jnp.zeros((tokens, WIDTH), F32)
    for part in range(4):
        columns = slice(part * WIDTH, (part + 1) * WIDTH)
        before_grad = (joined_grad[part].astype(F32) * slope_ref[:, columns]).astype(BF16)
        normed_grad += dot_nt(before_grad, joined_here[:, columns])
    grad = normalize_grad(rounded(normed_grad), normed, scale) + result_grad.astype(F32)
    grad = grad.astype(BF16)
    spread_grad = dot_nt(grad, lift_here[...])
    narrow_part = jnp.where(iota((tokens, LANES), 1) < 64, spread_grad[:, 384:], 0.0)
    left = jnp.where(
        kind == 2, spread_grad[:, :LANES], jnp.where(kind == 1, spread_grad[:, 256:384], narrow_part)
    )
    right = jnp.where(kind == 2, spread_grad[:, LANES:256], 0.0)
    row_grad = jnp.concatenate([left, right], axis=1).astype(BF16)
    term = dot_tn(spread, grad).reshape(devices // 2, CAP, WIDTH)
    term = jnp.stack([term[:, :, :256], term[:, :, 256:]], axis=1).reshape(devices, CAP, 256)
    placed = dot(one_hot(iota((amount, tokens), 0) == slot), row_grad).reshape(devices, CAP, 256)
    payload_ref[...] = jnp.concatenate([placed, term], axis=1).astype(BF16)


def sum_kernel(landed_ref, share_ref):
    total = jnp.sum(landed_ref[...].astype(F32), axis=0)[CAP:]
    share_ref[...] = jnp.broadcast_to(total[None].astype(BF16), share_ref.shape)


def scatter_kernel(landed_ref, code_ref, narrow_ref, middle_ref, wide_ref):
    sources = landed_ref.shape[0]
    amount = sources * CAP
    grads = landed_ref[...].astype(F32)[:, :CAP, :].reshape(amount, 256)
    code = code_ref[...]
    kind = code >> 11
    slab = code & 2047
    line = to_row(jnp.where(kind == 0, slab >> 1, slab))
    wide = jnp.where(kind == 2, grads, 0.0).astype(BF16)
    middle = jnp.where(kind == 1, grads[:, :LANES], 0.0).astype(BF16)
    narrow = jnp.where((kind == 0) & (iota((amount, LANES), 1) < 64), grads[:, :LANES], 0.0)
    narrow = jnp.where((slab & 1) == 1, pltpu.roll(narrow, 64, 1), narrow).astype(BF16)
    step = 256
    for start in range(0, wide_ref.shape[0], step):
        hot = one_hot(iota((step, amount), 0) + start == line)
        wide_ref[start : start + step, :] = dot(hot, wide)
        middle_ref[start : start + step, :] = dot(hot, middle)
        if start < narrow_ref.shape[0]:
            narrow_ref[start : start + step, :] = dot(hot, narrow)


def place_kernel(rank_ref, list_ref, kept_ref, arrived_ref, output_ref):
    traded = traded_slot(rank_ref, list_ref)
    output_ref[1 - traded] = kept_ref[...]
    output_ref[traded] = arrived_ref[...]


def delta_kernel(shares_ref, narrow_ref, middle_ref, wide_ref):
    devices = shares_ref.shape[0]
    shares = shares_ref[...].astype(F32).reshape(devices // 2, 2, CAP, 256)
    for half in range(2):
        columns = slice(half * 256, (half + 1) * 256)
        whole = shares[:, half].reshape(devices // 2 * CAP, 256)
        wide_ref[:, columns] = whole[:256]
        middle_ref[:, columns] = whole[256:384]
        narrow_ref[:, columns] = whole[384:448]


SMEM = pl.BlockSpec(memory_space=pltpu.SMEM)
VMEM = pl.BlockSpec(memory_space=pltpu.VMEM)
HBM = pl.BlockSpec(memory_space=pltpu.HBM)


def call(kernel, outs, args, scratch=(), flops=0, limit=32):
    shapes = [jax.ShapeDtypeStruct(shape, dtype) for shape, dtype in outs]
    arrays = [array for _, array in args]
    moved = sum(a.size * a.dtype.itemsize for a in arrays + shapes)
    return pl.pallas_call(
        kernel,
        out_shape=shapes,
        in_specs=[space for space, _ in args],
        out_specs=[VMEM] * len(shapes),
        scratch_shapes=list(scratch),
        cost_estimate=pl.CostEstimate(flops=flops, bytes_accessed=moved, transcendentals=0),
        compiler_params=pltpu.CompilerParams(vmem_limit_bytes=limit << 20),
    )(*arrays)


def exchange(array):
    return lax.all_to_all(array, ("dp", "table"), split_axis=0, concat_axis=0, tiled=True)


def body(
    history_lengths,
    balance_list,
    owner_device,
    owner_row,
    width_class,
    slab_index,
    narrow_table,
    middle_table,
    wide_table,
    narrow_lift,
    middle_lift,
    wide_lift,
    joined_weight,
    output_weight,
    cotangent,
):
    data_size = lax.axis_size("dp")
    table_size = lax.axis_size("table")
    devices = data_size * table_size
    rows = cotangent.shape[1]
    items = slab_index.shape[0]
    amount = devices * CAP
    data_rank = lax.axis_index("dp")
    self_rank = data_rank * table_size + lax.axis_index("table")
    rank = (SMEM, data_rank.reshape(1).astype(I32))
    plan = (SMEM, balance_list.T)
    owner = owner_device.transpose(0, 2, 1)
    class_list = width_class.reshape(-1, LANES)
    partners = [(i, i ^ (data_size // 2)) for i in range(data_size)]

    requests, slots = call(
        request_kernel,
        [((devices, CAP), I32), (owner_row.shape, I32)],
        [(VMEM, owner), (VMEM, owner_row)],
        flops=10**8,
    )
    asked = exchange(requests)
    (kinds,) = call(
        class_kernel,
        [((2 * rows, 1), I32)],
        [(VMEM, owner), (VMEM, owner_row), (VMEM, class_list)],
        flops=10**9,
    )
    (given_cotangent,) = call(
        give_kernel,
        [((rows, WIDTH), BF16)],
        [rank, plan, (HBM, cotangent)],
        scratch=[pltpu.SemaphoreType.DMA],
    )
    arrived_cotangent = lax.ppermute(given_cotangent, "dp", partners)
    own_classes = lax.dynamic_slice(class_list, (self_rank * (items // LANES), 0), (items // LANES, LANES))
    replies, codes = call(
        owner_kernel,
        [((amount, 256), BF16), ((amount, 1), I32)],
        [
            (VMEM, asked), (VMEM, own_classes), (VMEM, slab_index.reshape(-1, LANES)),
            (HBM, narrow_table), (HBM, middle_table), (HBM, wide_table),
        ],
        scratch=[
            pltpu.VMEM(narrow_table.shape, BF16),
            pltpu.VMEM(middle_table.shape, BF16),
            pltpu.VMEM(wide_table.shape, BF16),
            pltpu.SemaphoreType.DMA((3,)),
        ],
        flops=3 * 10**9,
    )
    landed = exchange(replies)
    kept_output, given_output, payload = call(
        layer_kernel,
        [((rows, WIDTH), BF16), ((rows, WIDTH), BF16), ((devices, 2 * CAP, 256), BF16)],
        [
            rank, plan, (SMEM, history_lengths.T), (VMEM, slots), (VMEM, landed), (VMEM, kinds),
            (HBM, cotangent), (HBM, arrived_cotangent), (HBM, narrow_lift), (HBM, middle_lift),
            (HBM, wide_lift), (HBM, joined_weight), (HBM, output_weight),
        ],
        scratch=[
            pltpu.VMEM((WIDTH, WIDTH), BF16),
            pltpu.VMEM((WIDTH, 4 * WIDTH), BF16),
            pltpu.VMEM((WIDTH, WIDTH), BF16),
            pltpu.VMEM((2, rows, WIDTH), BF16),
            pltpu.VMEM((2 * rows, 4 * WIDTH), F32),
            pltpu.VMEM((2, HEADS, rows, rows), F32),
            pltpu.SemaphoreType.DMA((7,)),
        ],
        flops=10**10,
        limit=40,
    )
    home = exchange(payload)
    (share,) = call(sum_kernel, [((devices, CAP, 256), BF16)], [(VMEM, home)])
    shares = exchange(share)
    given_output, _ = lax.optimization_barrier((given_output, share))
    arrived_output = lax.ppermute(given_output, "dp", partners)
    narrow_grad, middle_grad, wide_grad = call(
        scatter_kernel,
        [(narrow_table.shape, F32), (middle_table.shape, F32), (wide_table.shape, F32)],
        [(VMEM, home), (VMEM, codes)],
        flops=3 * 10**9,
    )
    (output,) = call(
        place_kernel, [(cotangent.shape, BF16)], [rank, plan, (VMEM, kept_output), (VMEM, arrived_output)]
    )
    narrow_delta, middle_delta, wide_delta = call(
        delta_kernel,
        [(narrow_lift.shape, F32), (middle_lift.shape, F32), (wide_lift.shape, F32)],
        [(VMEM, shares)],
    )
    return (output, narrow_grad, middle_grad, wide_grad, narrow_delta, middle_delta, wide_delta)


def solution(mesh):
    in_specs = (
        P(None, "table"),
        P(None, "table"),
        P(("dp", "table"), None, None),
        P(("dp", "table"), None),
        P(),
        P(("dp", "table")),
        P(("dp", "table"), None),
        P(("dp", "table"), None),
        P(("dp", "table"), None),
        P(),
        P(),
        P(),
        P(),
        P(),
        P(("dp", "table"), None, None),
    )
    out_specs = (
        P(("dp", "table"), None, None),
        P(("dp", "table"), None),
        P(("dp", "table"), None),
        P(("dp", "table"), None),
        P(),
        P(),
        P(),
    )
    return jax.shard_map(body, mesh=mesh, in_specs=in_specs, out_specs=out_specs, check_vma=False)
```

```python
import jax
import jax.numpy as jnp
from jax import lax
from jax.experimental import pallas as pl
from jax.experimental.pallas import tpu as pltpu
from jax.sharding import PartitionSpec as P

HEADS = 4
HEAD = 128
MAXLEN = 256
WIDTH = 512
CAP = 8
LANES = 128
OWNER_STEP = 256
LIMIT = 32

F32 = jnp.float32
BF16 = jnp.bfloat16
I32 = jnp.int32


def iota(shape, dim):
    return lax.broadcasted_iota(I32, shape, dim)


def one_hot(mask):
    return jnp.where(mask, 1.0, 0.0).astype(BF16)


def dot(a, b):
    return jnp.dot(a, b, preferred_element_type=F32)


def dot_nt(a, b):
    return lax.dot_general(a, b, (((1,), (1,)), ((), ())), preferred_element_type=F32)


def dot_tn(a, b):
    return lax.dot_general(a, b, (((0,), (0,)), ((), ())), preferred_element_type=F32)


def to_column(row):
    eye = iota((LANES, LANES), 0) == iota((LANES, LANES), 1)
    parts = []
    for start in range(0, row.shape[1], LANES):
        piece = row[:, start : start + LANES].astype(F32)
        parts.append(jnp.sum(jnp.where(eye, piece, 0.0), axis=1, keepdims=True))
    return jnp.concatenate(parts, axis=0).astype(I32)


def to_row(column):
    eye = iota((LANES, LANES), 0) == iota((LANES, LANES), 1)
    parts = []
    for start in range(0, column.shape[0], LANES):
        piece = column[start : start + LANES].astype(F32)
        parts.append(jnp.sum(jnp.where(eye, piece, 0.0), axis=0, keepdims=True))
    return jnp.concatenate(parts, axis=1).astype(I32)


def lane_sum(mask, values):
    return jnp.sum(jnp.where(mask, values, 0.0), axis=1, keepdims=True).astype(I32)


def flat_row(ref):
    return jnp.concatenate([ref[0:1, :], ref[1:2, :]], axis=1)


def request_kernel(owner_ref, item_ref, request_ref, slot_ref):
    devices = request_ref.shape[0]
    owner = jnp.concatenate([owner_ref[0], owner_ref[1]], axis=1)
    item = flat_row(item_ref)
    tokens = owner.shape[1]
    named = iota((devices, tokens), 0) == owner
    hot = one_hot(named)
    earlier = one_hot(iota((tokens, tokens), 0) < iota((tokens, tokens), 1))
    before = dot(hot, earlier)
    rank = jnp.sum(jnp.where(named, before, 0.0), axis=0, keepdims=True).astype(I32)
    place = iota((2 * CAP, tokens), 0)
    value = jnp.where(place < CAP, item >> 6, item & 63)
    table = jnp.where((place & (CAP - 1)) == rank, value, 0).astype(F32).astype(BF16)
    filled = dot_nt(hot, table).astype(I32)
    request_ref[...] = filled[:, :CAP] * 64 + filled[:, CAP:]
    slot = owner * CAP + rank
    half = tokens // 2
    slot_ref[0:1, :] = slot[:, :half]
    slot_ref[1:2, :] = slot[:, half:]


def class_kernel(owner_ref, item_ref, class_list_ref, class_ref, list_here, copied):
    copy = pltpu.make_async_copy(class_list_ref, list_here, copied)
    copy.start()
    item = to_column(flat_row(item_ref))
    owner = jnp.concatenate([owner_ref[0], owner_ref[1]], axis=1)
    line = to_column(owner) * (4096 // LANES) + (item >> 7)
    tokens = line.shape[0]
    lines = class_list_ref.shape[0]
    step = 512
    total = jnp.zeros((tokens, LANES), F32)
    copy.wait()
    for start in range(0, lines, step):
        hot = one_hot(iota((tokens, step), 1) + start == line)
        total += dot(hot, list_here[start : start + step, :].astype(F32).astype(BF16))
    kind = to_row(lane_sum(iota((tokens, LANES), 1) == (item & 127), total))
    class_ref[0:1, :] = kind[:, : tokens // 2]
    class_ref[1:2, :] = kind[:, tokens // 2 :]


def request_codes(asked_ref, marks):
    asked = asked_ref[...]
    sources = asked.shape[0]
    amount = sources * CAP
    expand = one_hot((iota((amount, sources), 0) >> 3) == iota((amount, sources), 1))
    mine = (iota((amount, CAP), 0) & (CAP - 1)) == iota((amount, CAP), 1)
    high = lane_sum(mine, dot(expand, (asked >> 7).astype(F32).astype(BF16)))
    low = lane_sum(mine, dot(expand, (asked & 127).astype(F32).astype(BF16)))
    found = dot(one_hot(iota((amount, marks.shape[0]), 1) == high), marks)
    mine = iota((amount, LANES), 1) == low
    return lane_sum(mine, found[:, LANES:]) * LANES + lane_sum(mine, found[:, :LANES])


def stage_rows_kernel(
    rank_ref, after_ref, class_list_ref, slab_ref, narrow_ref, middle_ref, wide_ref, table_ref, marks_ref,
    class_here, slab_here, copied,
):
    del after_ref
    groups = slab_here.shape[0]
    lines = narrow_ref.shape[0]
    moves = [
        (class_list_ref.at[pl.ds(pl.multiple_of(rank_ref[1] * groups, groups), groups)], class_here),
        (slab_ref, slab_here),
        (wide_ref, table_ref.at[:, 0:256]),
        (middle_ref, table_ref.at[:, 256:384]),
        (narrow_ref, table_ref.at[0:lines, 384:512]),
    ]
    copies = [pltpu.make_async_copy(there, here, copied.at[k]) for k, (there, here) in enumerate(moves)]
    for copy in copies:
        copy.start()
    table_ref[lines:, 384:] = jnp.zeros((table_ref.shape[0] - lines, LANES), BF16)
    for copy in copies:
        copy.wait()
    slab = slab_here[...]
    marks = jnp.concatenate([slab & 127, (slab >> 7) + 16 * class_here[...]], axis=1)
    marks_ref[...] = marks.astype(F32).astype(BF16)


def owner_kernel(asked_ref, marks_ref, table_ref, reply_ref):
    amount = reply_ref.shape[0]
    code = request_codes(asked_ref, marks_ref[...])
    kind = code >> 11
    slab = code & 2047
    line = jnp.where(kind == 0, slab >> 1, slab)
    lines = table_ref.shape[0]
    for start in range(0, amount, OWNER_STEP):
        rows = slice(start, start + OWNER_STEP)
        hot = one_hot(iota((OWNER_STEP, lines), 1) == line[rows])
        here = kind[rows]
        side = dot(hot, table_ref[:, 256:])
        narrow = side[:, LANES:]
        narrow = jnp.where((slab[rows] & 1) == 1, pltpu.roll(narrow, 64, 1), narrow)
        narrow = jnp.where(iota((OWNER_STEP, LANES), 1) < 64, narrow, 0.0)
        side = jnp.where(here == 1, side[:, :LANES], narrow)
        wide = dot(hot, table_ref[:, :256])
        left = jnp.where(here == 2, wide[:, :LANES], side)
        right = jnp.where(here == 2, wide[:, LANES:], 0.0)
        reply_ref[rows, :] = jnp.concatenate([left, right], axis=1).astype(BF16)


def traded_slot(rank_ref, list_ref):
    rank = rank_ref[0]
    return jnp.where((list_ref[0, rank] >> 1) != rank, 0, 1)


def stage_layer_kernel(
    after_ref, narrow_ref, middle_ref, wide_ref, joined_ref, lift_here, gating_here, values_here, copied
):
    del after_ref
    moves = [
        (wide_ref, lift_here.at[0:256]),
        (middle_ref, lift_here.at[256:384]),
        (narrow_ref, lift_here.at[384:448]),
    ]
    for part, here in enumerate([gating_here, values_here]):
        moves.append((joined_ref.at[:, part * WIDTH : (part + 1) * WIDTH], here))
    copies = [pltpu.make_async_copy(there, here, copied.at[k]) for k, (there, here) in enumerate(moves)]
    for copy in copies:
        copy.start()
    lift_here[448:, :] = jnp.zeros((64, WIDTH), BF16)
    for copy in copies:
        copy.wait()


def mean(values):
    return jnp.sum(values, axis=1, keepdims=True) * (1.0 / WIDTH)


def normalize(values):
    centre = values - mean(values)
    scale = lax.rsqrt(mean(centre * centre) + 1e-06)
    return centre * scale, scale


def normalize_grad(grad, normed, scale):
    return scale * (grad - mean(grad) - normed * mean(grad * normed))


def sigmoid(values):
    return 0.5 * jnp.tanh(0.5 * values) + 0.5


def rounded(values):
    return values.astype(BF16).astype(F32)


def layer_kernel(
    rank_ref, list_ref, length_ref, slot_ref, landed_ref, class_ref, lift_here, gating_here, values_here,
    cotangent_ref, arrived_ref, joined_ref, output_weight_ref, kept_ref, given_ref, payload_ref,
    queries_here, keys_here, output_here, cotangent_here, slope_ref, curve_ref, copied,
):
    rank = rank_ref[0]
    traded = traded_slot(rank_ref, list_ref)
    kept = 1 - traded
    moves = [
        (joined_ref.at[:, 2 * WIDTH : 3 * WIDTH], queries_here),
        (joined_ref.at[:, 3 * WIDTH :], keys_here),
        (output_weight_ref, output_here),
        (cotangent_ref.at[kept], cotangent_here.at[kept]),
        (arrived_ref.at[list_ref[traded, rank] & 1], cotangent_here.at[traded]),
    ]
    copies = [pltpu.make_async_copy(there, here, copied.at[k]) for k, (there, here) in enumerate(moves)]
    for copy in copies:
        copy.start()
    zero = jnp.zeros((), BF16)
    rows = kept_ref.shape[0]
    hists = slot_ref.shape[0]
    tokens = hists * rows
    devices = payload_ref.shape[0]
    amount = devices * CAP
    slot = flat_row(slot_ref)
    raw = dot(one_hot(iota((tokens, amount), 1) == to_column(slot)), landed_ref[...]).astype(BF16)
    kind = to_column(flat_row(class_ref))
    spread = jnp.concatenate(
        [
            jnp.where(kind == 2, raw, zero),
            jnp.where(kind == 1, raw[:, :LANES], zero),
            jnp.where(kind == 0, raw[:, :LANES], zero),
        ],
        axis=1,
    )
    widened = rounded(dot(spread, lift_here[...]))
    normed, scale = normalize(widened)
    normed_low = normed.astype(BF16)
    joined_here = [gating_here, values_here, queries_here, keys_here]
    joined = []
    for part in range(4):
        columns = slice(part * WIDTH, (part + 1) * WIDTH)
        if part >= 2:
            copies[part - 2].wait()
        before = dot(normed_low, joined_here[part][...])
        gate = sigmoid(before)
        joined.append((before * gate).astype(BF16))
        slope_ref[:, columns] = gate * (1.0 + before * (1.0 - gate))
    gating, values, queries, keys = joined
    gating = gating.astype(F32)
    place = iota((tokens, 1), 0)
    lengths = [length_ref[hist, rank] for hist in range(hists)]
    valid = place < jnp.where(place < rows, lengths[0], rows + lengths[1])
    across = iota((rows, rows), 1)
    causal = across <= iota((rows, rows), 0)
    weights = {}
    mixed = []
    for hist in range(hists):
        lines = slice(hist * rows, (hist + 1) * rows)
        factor = jnp.where(causal & (across < lengths[hist]), 1.0 / MAXLEN, 0.0)
        heads = []
        for head in range(HEADS):
            columns = slice(head * HEAD, (head + 1) * HEAD)
            scores = dot_nt(queries[lines, columns], keys[lines, columns])
            gate = sigmoid(scores)
            scaled = gate * factor
            weights[hist, head] = (scores * scaled).astype(BF16)
            curve_ref[hist, head] = scaled * (1.0 + scores * (1.0 - gate))
            heads.append(dot(weights[hist, head], values[lines, columns]))
        mixed.append(jnp.concatenate(heads, axis=1))
    mixed_normed, mixed_scale = normalize(jnp.concatenate(mixed, axis=0))
    gated = (mixed_normed * gating).astype(BF16)
    for copy in copies[2:]:
        copy.wait()
    result = dot(gated, output_here[...]) + widened
    output = jnp.where(valid, result, 0.0).astype(BF16)
    kept_ref[...] = jnp.where(traded == 0, output[rows:], output[:rows])
    given_ref[...] = jnp.where(traded == 0, output[:rows], output[rows:])

    cotangent = jnp.concatenate([cotangent_here[0], cotangent_here[1]], axis=0)
    result_grad = jnp.where(valid, cotangent, zero)
    gated_grad = rounded(dot_nt(result_grad, output_here[...]))
    gating_grad = (gated_grad * mixed_normed).astype(BF16)
    mixed_grad = normalize_grad(gated_grad * gating, mixed_normed, mixed_scale).astype(BF16)
    grads = [[], [], []]
    for hist in range(hists):
        lines = slice(hist * rows, (hist + 1) * rows)
        heads = [[], [], []]
        for head in range(HEADS):
            columns = slice(head * HEAD, (head + 1) * HEAD)
            own = mixed_grad[lines, columns]
            weights_grad = rounded(dot_nt(own, values[lines, columns]))
            scores_grad = (weights_grad * curve_ref[hist, head]).astype(BF16)
            heads[0].append(dot_tn(weights[hist, head], own))
            heads[1].append(dot(scores_grad, keys[lines, columns]))
            heads[2].append(dot_tn(scores_grad, queries[lines, columns]))
        for part in range(3):
            grads[part].append(jnp.concatenate(heads[part], axis=1).astype(BF16))
    joined_grad = [gating_grad] + [jnp.concatenate(g, axis=0) for g in grads]
    normed_grad = jnp.zeros((tokens, WIDTH), F32)
    for part in range(4):
        columns = slice(part * WIDTH, (part + 1) * WIDTH)
        before_grad = (joined_grad[part].astype(F32) * slope_ref[:, columns]).astype(BF16)
        normed_grad += dot_nt(before_grad, joined_here[part][...])
    grad = normalize_grad(rounded(normed_grad), normed, scale) + result_grad.astype(F32)
    grad = grad.astype(BF16)
    spread_grad = dot_nt(grad, lift_here[...])
    narrow_part = jnp.where(iota((tokens, LANES), 1) < 64, spread_grad[:, 384:], 0.0)
    left = jnp.where(
        kind == 2, spread_grad[:, :LANES], jnp.where(kind == 1, spread_grad[:, 256:384], narrow_part)
    )
    right = jnp.where(kind == 2, spread_grad[:, LANES:256], 0.0)
    row_grad = jnp.concatenate([left, right], axis=1).astype(BF16)
    term = dot_tn(spread, grad).reshape(devices // 2, CAP, WIDTH)
    term = jnp.stack([term[:, :, :256], term[:, :, 256:]], axis=1).reshape(devices, CAP, 256)
    placed = dot(one_hot(iota((amount, tokens), 0) == slot), row_grad).reshape(devices, CAP, 256)
    payload_ref[...] = jnp.concatenate([placed, term], axis=1).astype(BF16)


def sum_kernel(landed_ref, share_ref):
    total = jnp.sum(landed_ref[...].astype(F32), axis=0)[CAP:]
    share_ref[...] = jnp.broadcast_to(total[None].astype(BF16), share_ref.shape)


def scatter_kernel(landed_ref, asked_ref, marks_ref, narrow_ref, middle_ref, wide_ref):
    sources = landed_ref.shape[0]
    amount = sources * CAP
    grads = landed_ref[...].astype(F32)[:, :CAP, :].reshape(amount, 256)
    code = request_codes(asked_ref, marks_ref[...])
    kind = code >> 11
    slab = code & 2047
    line = to_row(jnp.where(kind == 0, slab >> 1, slab))
    wide = jnp.where(kind == 2, grads, 0.0).astype(BF16)
    middle = jnp.where(kind == 1, grads[:, :LANES], 0.0).astype(BF16)
    narrow = jnp.where((kind == 0) & (iota((amount, LANES), 1) < 64), grads[:, :LANES], 0.0)
    narrow = jnp.where((slab & 1) == 1, pltpu.roll(narrow, 64, 1), narrow).astype(BF16)
    step = 256
    for start in range(0, wide_ref.shape[0], step):
        hot = one_hot(iota((step, amount), 0) + start == line)
        wide_ref[start : start + step, :] = dot(hot, wide)
        middle_ref[start : start + step, :] = dot(hot, middle)
        if start < narrow_ref.shape[0]:
            narrow_ref[start : start + step, :] = dot(hot, narrow)


def finish_kernel(
    rank_ref, list_ref, kept_ref, arrived_ref, shares_ref, output_ref, narrow_ref, middle_ref, wide_ref
):
    traded = traded_slot(rank_ref, list_ref)
    output_ref[1 - traded] = kept_ref[...]
    output_ref[traded] = arrived_ref[...]
    devices = shares_ref.shape[0]
    shares = shares_ref[...].astype(F32).reshape(devices // 2, 2, CAP, 256)
    for half in range(2):
        columns = slice(half * 256, (half + 1) * 256)
        whole = shares[:, half].reshape(devices // 2 * CAP, 256)
        wide_ref[:, columns] = whole[:256]
        middle_ref[:, columns] = whole[256:384]
        narrow_ref[:, columns] = whole[384:448]


SMEM = pl.BlockSpec(memory_space=pltpu.SMEM)
VMEM = pl.BlockSpec(memory_space=pltpu.VMEM)
HBM = pl.BlockSpec(memory_space=pltpu.HBM)
KEPT = pl.BlockSpec(memory_space=pltpu.VMEM)


def call(kernel, outs, args, scratch=(), flops=0, limit=LIMIT):
    arrays = []
    for space, array in args:
        if space is KEPT:
            array = pltpu.with_memory_space_constraint(array, pltpu.VMEM)
        elif space is not VMEM:
            array = pltpu.with_memory_space_constraint(array, pltpu.HBM)
        arrays.append(array)
    shapes = [
        pltpu.VMEM(out[0], out[1]) if KEPT in out[2:] else jax.ShapeDtypeStruct(out[0], out[1]) for out in outs
    ]
    moved = sum(a.size * a.dtype.itemsize for _, a in args)
    return pl.pallas_call(
        kernel,
        out_shape=shapes,
        in_specs=[space for space, _ in args],
        out_specs=[VMEM] * len(shapes),
        scratch_shapes=list(scratch),
        cost_estimate=pl.CostEstimate(flops=flops, bytes_accessed=moved, transcendentals=0),
        compiler_params=pltpu.CompilerParams(vmem_limit_bytes=int(limit * 2**20)),
    )(*arrays)


def exchange(array):
    return lax.all_to_all(array, ("dp", "table"), split_axis=0, concat_axis=0, tiled=True)


def body(
    history_lengths,
    balance_list,
    owner_device,
    owner_row,
    width_class,
    slab_index,
    narrow_table,
    middle_table,
    wide_table,
    narrow_lift,
    middle_lift,
    wide_lift,
    joined_weight,
    output_weight,
    cotangent,
):
    data_size = lax.axis_size("dp")
    table_size = lax.axis_size("table")
    devices = data_size * table_size
    rows = cotangent.shape[1]
    amount = devices * CAP
    data_rank = lax.axis_index("dp")
    self_rank = data_rank * table_size + lax.axis_index("table")
    rank = (SMEM, jnp.stack([data_rank, self_rank]).astype(I32))
    plan = (SMEM, balance_list.T)
    owner = owner_device.transpose(0, 2, 1)
    class_list = width_class.reshape(-1, LANES)
    partners = [(i, i ^ (data_size // 2)) for i in range(data_size)]

    requests, slots = call(
        request_kernel,
        [((devices, CAP), I32), (owner_row.shape, I32)],
        [(VMEM, owner), (VMEM, owner_row)],
        flops=10**8,
        limit=62,
    )
    asked = exchange(requests)
    slab_list = slab_index.reshape(-1, LANES)
    ready_cotangent, slots = lax.optimization_barrier((cotangent, slots))
    arrived_cotangent = lax.ppermute(ready_cotangent, "dp", partners)
    table, marks = call(
        stage_rows_kernel,
        [((middle_table.shape[0], 512), BF16, KEPT), ((slab_list.shape[0], 256), BF16, KEPT)],
        [
            rank, (HBM, slots), (HBM, class_list), (HBM, slab_list),
            (HBM, narrow_table), (HBM, middle_table), (HBM, wide_table),
        ],
        scratch=[
            pltpu.VMEM(slab_list.shape, I32), pltpu.VMEM(slab_list.shape, I32), pltpu.SemaphoreType.DMA((5,)),
        ],
    )
    (replies,) = call(
        owner_kernel,
        [((amount, 256), BF16)],
        [(VMEM, asked), (KEPT, marks), (KEPT, table)],
        flops=3 * 10**9,
    )
    replies, arrived_cotangent = lax.optimization_barrier((replies, arrived_cotangent))
    landed = exchange(replies)
    (kinds,) = call(
        class_kernel,
        [(owner_row.shape, I32)],
        [(VMEM, owner), (VMEM, owner_row), (HBM, class_list)],
        scratch=[pltpu.VMEM(class_list.shape, I32), pltpu.SemaphoreType.DMA],
        flops=10**9,
    )
    staged = call(
        stage_layer_kernel,
        [((WIDTH, WIDTH), BF16, KEPT)] * 3,
        [(HBM, slots), (HBM, narrow_lift), (HBM, middle_lift), (HBM, wide_lift), (HBM, joined_weight)],
        scratch=[pltpu.SemaphoreType.DMA((5,))],
    )
    kept_output, given_output, payload = call(
        layer_kernel,
        [((rows, WIDTH), BF16), ((rows, WIDTH), BF16), ((devices, 2 * CAP, 256), BF16)],
        [rank, plan, (SMEM, history_lengths.T), (VMEM, slots), (VMEM, landed), (VMEM, kinds)]
        + [(KEPT, array) for array in staged]
        + [(HBM, cotangent), (VMEM, arrived_cotangent), (HBM, joined_weight), (HBM, output_weight)],
        scratch=[
            pltpu.VMEM((WIDTH, WIDTH), BF16),
            pltpu.VMEM((WIDTH, WIDTH), BF16),
            pltpu.VMEM((WIDTH, WIDTH), BF16),
            pltpu.VMEM((2, rows, WIDTH), BF16),
            pltpu.VMEM((2 * rows, 4 * WIDTH), F32),
            pltpu.VMEM((2, HEADS, rows, rows), F32),
            pltpu.SemaphoreType.DMA((5,)),
        ],
        flops=10**10,
    )
    home = exchange(payload)
    (share,) = call(sum_kernel, [((devices, CAP, 256), BF16)], [(VMEM, home)])
    shares = exchange(share)
    given_output, _ = lax.optimization_barrier((given_output, share))
    arrived_output = lax.ppermute(given_output, "dp", partners)
    narrow_grad, middle_grad, wide_grad = call(
        scatter_kernel,
        [(narrow_table.shape, F32), (middle_table.shape, F32), (wide_table.shape, F32)],
        [(VMEM, home), (VMEM, asked), (KEPT, marks)],
        flops=3 * 10**9,
    )
    output, narrow_delta, middle_delta, wide_delta = call(
        finish_kernel,
        [
            (cotangent.shape, BF16), (narrow_lift.shape, F32), (middle_lift.shape, F32), (wide_lift.shape, F32),
        ],
        [rank, plan, (VMEM, kept_output), (VMEM, arrived_output), (VMEM, shares)],
    )
    return (output, narrow_grad, middle_grad, wide_grad, narrow_delta, middle_delta, wide_delta)


def solution(mesh):
    in_specs = (
        P(None, "table"),
        P(None, "table"),
        P(("dp", "table"), None, None),
        P(("dp", "table"), None),
        P(),
        P(("dp", "table")),
        P(("dp", "table"), None),
        P(("dp", "table"), None),
        P(("dp", "table"), None),
        P(),
        P(),
        P(),
        P(),
        P(),
        P(("dp", "table"), None, None),
    )
    out_specs = (
        P(("dp", "table"), None, None),
        P(("dp", "table"), None),
        P(("dp", "table"), None),
        P(("dp", "table"), None),
        P(),
        P(),
        P(),
    )
    return jax.shard_map(body, mesh=mesh, in_specs=in_specs, out_specs=out_specs, check_vma=False)
```

```python
import jax
import jax.numpy as jnp
from jax import lax
from jax.experimental import pallas as pl
from jax.experimental.pallas import tpu as pltpu
from jax.sharding import PartitionSpec as P

HEADS = 4
HEAD = 128
MAXLEN = 256
WIDTH = 512
CAP = 8
LANES = 128
OWNER_STEP = 256
LIMIT = 32

F32 = jnp.float32
BF16 = jnp.bfloat16
I32 = jnp.int32


def iota(shape, dim):
    return lax.broadcasted_iota(I32, shape, dim)


def one_hot(mask):
    return jnp.where(mask, 1.0, 0.0).astype(BF16)


def dot(a, b):
    return jnp.dot(a, b, preferred_element_type=F32)


def dot_nt(a, b):
    return lax.dot_general(a, b, (((1,), (1,)), ((), ())), preferred_element_type=F32)


def dot_tn(a, b):
    return lax.dot_general(a, b, (((0,), (0,)), ((), ())), preferred_element_type=F32)


def to_column(row):
    eye = iota((LANES, LANES), 0) == iota((LANES, LANES), 1)
    parts = []
    for start in range(0, row.shape[1], LANES):
        piece = row[:, start : start + LANES].astype(F32)
        parts.append(jnp.sum(jnp.where(eye, piece, 0.0), axis=1, keepdims=True))
    return jnp.concatenate(parts, axis=0).astype(I32)


def to_row(column):
    eye = iota((LANES, LANES), 0) == iota((LANES, LANES), 1)
    parts = []
    for start in range(0, column.shape[0], LANES):
        piece = column[start : start + LANES].astype(F32)
        parts.append(jnp.sum(jnp.where(eye, piece, 0.0), axis=0, keepdims=True))
    return jnp.concatenate(parts, axis=1).astype(I32)


def lane_sum(mask, values):
    return jnp.sum(jnp.where(mask, values, 0.0), axis=1, keepdims=True).astype(I32)


def flat_row(ref):
    return jnp.concatenate([ref[0:1, :], ref[1:2, :]], axis=1)


def request_kernel(owner_ref, item_ref, request_ref, slot_ref):
    devices = request_ref.shape[0]
    owner = jnp.concatenate([owner_ref[0], owner_ref[1]], axis=1)
    item = flat_row(item_ref)
    tokens = owner.shape[1]
    named = iota((devices, tokens), 0) == owner
    hot = one_hot(named)
    earlier = one_hot(iota((tokens, tokens), 0) < iota((tokens, tokens), 1))
    before = dot(hot, earlier)
    rank = jnp.sum(jnp.where(named, before, 0.0), axis=0, keepdims=True).astype(I32)
    place = iota((2 * CAP, tokens), 0)
    value = jnp.where(place < CAP, item >> 6, item & 63)
    table = jnp.where((place & (CAP - 1)) == rank, value, 0).astype(F32).astype(BF16)
    filled = dot_nt(hot, table).astype(I32)
    request_ref[...] = filled[:, :CAP] * 64 + filled[:, CAP:]
    slot = owner * CAP + rank
    half = tokens // 2
    slot_ref[0:1, :] = slot[:, :half]
    slot_ref[1:2, :] = slot[:, half:]


def class_kernel(owner_ref, item_ref, class_list_ref, class_ref, list_here, copied):
    copy = pltpu.make_async_copy(class_list_ref, list_here, copied)
    copy.start()
    item = to_column(flat_row(item_ref))
    owner = jnp.concatenate([owner_ref[0], owner_ref[1]], axis=1)
    line = to_column(owner) * (4096 // LANES) + (item >> 7)
    tokens = line.shape[0]
    lines = class_list_ref.shape[0]
    step = 512
    total = jnp.zeros((tokens, LANES), F32)
    copy.wait()
    for start in range(0, lines, step):
        hot = one_hot(iota((tokens, step), 1) + start == line)
        total += dot(hot, list_here[start : start + step, :].astype(F32).astype(BF16))
    kind = to_row(lane_sum(iota((tokens, LANES), 1) == (item & 127), total))
    class_ref[0:1, :] = kind[:, : tokens // 2]
    class_ref[1:2, :] = kind[:, tokens // 2 :]


def request_codes(asked_ref, marks):
    asked = asked_ref[...]
    sources = asked.shape[0]
    amount = sources * CAP
    expand = one_hot((iota((amount, sources), 0) >> 3) == iota((amount, sources), 1))
    mine = (iota((amount, CAP), 0) & (CAP - 1)) == iota((amount, CAP), 1)
    high = lane_sum(mine, dot(expand, (asked >> 7).astype(F32).astype(BF16)))
    low = lane_sum(mine, dot(expand, (asked & 127).astype(F32).astype(BF16)))
    found = dot(one_hot(iota((amount, marks.shape[0]), 1) == high), marks)
    mine = iota((amount, LANES), 1) == low
    return lane_sum(mine, found[:, LANES:]) * LANES + lane_sum(mine, found[:, :LANES])


def stage_rows_kernel(
    rank_ref, after_ref, class_list_ref, slab_ref, narrow_ref, middle_ref, wide_ref, table_ref, marks_ref,
    class_here, slab_here, copied,
):
    del after_ref
    groups = slab_here.shape[0]
    lines = narrow_ref.shape[0]
    moves = [
        (class_list_ref.at[pl.ds(pl.multiple_of(rank_ref[1] * groups, groups), groups)], class_here),
        (slab_ref, slab_here),
        (wide_ref, table_ref.at[:, 0:256]),
        (middle_ref, table_ref.at[:, 256:384]),
        (narrow_ref, table_ref.at[0:lines, 384:512]),
    ]
    copies = [pltpu.make_async_copy(there, here, copied.at[k]) for k, (there, here) in enumerate(moves)]
    for copy in copies:
        copy.start()
    table_ref[lines:, 384:] = jnp.zeros((table_ref.shape[0] - lines, LANES), BF16)
    for copy in copies:
        copy.wait()
    slab = slab_here[...]
    marks = jnp.concatenate([slab & 127, (slab >> 7) + 16 * class_here[...]], axis=1)
    marks_ref[...] = marks.astype(F32).astype(BF16)


def owner_kernel(asked_ref, marks_ref, table_ref, reply_ref):
    amount = reply_ref.shape[0]
    code = request_codes(asked_ref, marks_ref[...])
    kind = code >> 11
    slab = code & 2047
    line = jnp.where(kind == 0, slab >> 1, slab)
    lines = table_ref.shape[0]
    for start in range(0, amount, OWNER_STEP):
        rows = slice(start, start + OWNER_STEP)
        hot = one_hot(iota((OWNER_STEP, lines), 1) == line[rows])
        here = kind[rows]
        side = dot(hot, table_ref[:, 256:])
        narrow = side[:, LANES:]
        narrow = jnp.where((slab[rows] & 1) == 1, pltpu.roll(narrow, 64, 1), narrow)
        narrow = jnp.where(iota((OWNER_STEP, LANES), 1) < 64, narrow, 0.0)
        side = jnp.where(here == 1, side[:, :LANES], narrow)
        wide = dot(hot, table_ref[:, :256])
        left = jnp.where(here == 2, wide[:, :LANES], side)
        right = jnp.where(here == 2, wide[:, LANES:], 0.0)
        reply_ref[rows, :] = jnp.concatenate([left, right], axis=1).astype(BF16)


def traded_slot(rank_ref, list_ref):
    rank = rank_ref[0]
    return jnp.where((list_ref[0, rank] >> 1) != rank, 0, 1)


def stage_layer_kernel(
    after_ref, narrow_ref, middle_ref, wide_ref, joined_ref, lift_here, gating_here, values_here, copied
):
    del after_ref
    moves = [
        (wide_ref, lift_here.at[0:256]),
        (middle_ref, lift_here.at[256:384]),
        (narrow_ref, lift_here.at[384:448]),
    ]
    for part, here in enumerate([gating_here, values_here]):
        moves.append((joined_ref.at[:, part * WIDTH : (part + 1) * WIDTH], here))
    copies = [pltpu.make_async_copy(there, here, copied.at[k]) for k, (there, here) in enumerate(moves)]
    for copy in copies:
        copy.start()
    lift_here[448:, :] = jnp.zeros((64, WIDTH), BF16)
    for copy in copies:
        copy.wait()


def mean(values):
    return jnp.sum(values, axis=1, keepdims=True) * (1.0 / WIDTH)


def normalize(values):
    centre = values - mean(values)
    scale = lax.rsqrt(mean(centre * centre) + 1e-06)
    return centre * scale, scale


def normalize_grad(grad, normed, scale):
    return scale * (grad - mean(grad) - normed * mean(grad * normed))


def sigmoid(values):
    return 0.5 * jnp.tanh(0.5 * values) + 0.5


def rounded(values):
    return values.astype(BF16).astype(F32)


def layer_kernel(
    rank_ref, list_ref, length_ref, slot_ref, landed_ref, class_ref, lift_here, gating_here, values_here,
    cotangent_ref, arrived_ref, joined_ref, output_weight_ref, kept_ref, given_ref, payload_ref,
    queries_here, keys_here, output_here, cotangent_here, slope_ref, curve_ref, copied,
):
    rank = rank_ref[0]
    traded = traded_slot(rank_ref, list_ref)
    kept = 1 - traded
    moves = [
        (joined_ref.at[:, 2 * WIDTH : 3 * WIDTH], queries_here),
        (joined_ref.at[:, 3 * WIDTH :], keys_here),
        (output_weight_ref, output_here),
        (cotangent_ref.at[kept], cotangent_here.at[kept]),
        (arrived_ref.at[list_ref[traded, rank] & 1], cotangent_here.at[traded]),
    ]
    copies = [pltpu.make_async_copy(there, here, copied.at[k]) for k, (there, here) in enumerate(moves)]
    for copy in copies:
        copy.start()
    zero = jnp.zeros((), BF16)
    rows = kept_ref.shape[0]
    hists = slot_ref.shape[0]
    tokens = hists * rows
    devices = payload_ref.shape[0]
    amount = devices * CAP
    slot = flat_row(slot_ref)
    placing = one_hot(iota((amount, tokens), 0) == slot)
    raw = dot_tn(placing, landed_ref[...]).astype(BF16)
    kind = to_column(flat_row(class_ref))
    spread = jnp.concatenate(
        [
            jnp.where(kind == 2, raw, zero),
            jnp.where(kind == 1, raw[:, :LANES], zero),
            jnp.where(kind == 0, raw[:, :LANES], zero),
        ],
        axis=1,
    )
    widened = rounded(dot(spread, lift_here[...]))
    normed, scale = normalize(widened)
    normed_low = normed.astype(BF16)
    for copy in copies:
        copy.wait()
    joined_here = [gating_here, values_here, queries_here, keys_here]
    joined = []
    for part in range(4):
        columns = slice(part * WIDTH, (part + 1) * WIDTH)
        before = dot(normed_low, joined_here[part][...])
        gate = sigmoid(before)
        active = before * gate
        joined.append(active.astype(BF16))
        slope_ref[:, columns] = gate + active * (1.0 - gate)
    gating, values, queries, keys = joined
    gating = gating.astype(F32)
    place = iota((tokens, 1), 0)
    lengths = [length_ref[hist, rank] for hist in range(hists)]
    valid = place < jnp.where(place < rows, lengths[0], rows + lengths[1])
    across = iota((rows, rows), 1)
    causal = across <= iota((rows, rows), 0)
    weights = {}
    mixed = []
    for hist in range(hists):
        lines = slice(hist * rows, (hist + 1) * rows)
        factor = jnp.where(causal & (across < lengths[hist]), 1.0 / MAXLEN, 0.0)
        heads = []
        for head in range(HEADS):
            columns = slice(head * HEAD, (head + 1) * HEAD)
            scores = dot_nt(queries[lines, columns], keys[lines, columns])
            gate = sigmoid(scores)
            scaled = gate * factor
            active = scores * scaled
            weights[hist, head] = active.astype(BF16)
            curve_ref[hist, head] = scaled + active * (1.0 - gate)
            heads.append(dot(weights[hist, head], values[lines, columns]))
        mixed.append(jnp.concatenate(heads, axis=1))
    mixed_normed, mixed_scale = normalize(jnp.concatenate(mixed, axis=0))
    gated = (mixed_normed * gating).astype(BF16)
    result = dot(gated, output_here[...]) + widened
    output = jnp.where(valid, result, 0.0).astype(BF16)
    kept_ref[...] = jnp.where(traded == 0, output[rows:], output[:rows])
    given_ref[...] = jnp.where(traded == 0, output[:rows], output[rows:])

    cotangent = jnp.concatenate([cotangent_here[0], cotangent_here[1]], axis=0)
    result_grad = jnp.where(valid, cotangent, zero)
    gated_grad = rounded(dot_nt(result_grad, output_here[...]))
    gating_grad = (gated_grad * mixed_normed).astype(BF16)
    mixed_grad = normalize_grad(gated_grad * gating, mixed_normed, mixed_scale).astype(BF16)
    grads = [[], [], []]
    for hist in range(hists):
        lines = slice(hist * rows, (hist + 1) * rows)
        heads = [[], [], []]
        for head in range(HEADS):
            columns = slice(head * HEAD, (head + 1) * HEAD)
            own = mixed_grad[lines, columns]
            weights_grad = rounded(dot_nt(own, values[lines, columns]))
            scores_grad = (weights_grad * curve_ref[hist, head]).astype(BF16)
            heads[0].append(dot_tn(weights[hist, head], own))
            heads[1].append(dot(scores_grad, keys[lines, columns]))
            heads[2].append(dot_tn(scores_grad, queries[lines, columns]))
        for part in range(3):
            grads[part].append(jnp.concatenate(heads[part], axis=1).astype(BF16))
    joined_grad = [gating_grad] + [jnp.concatenate(g, axis=0) for g in grads]
    normed_grad = jnp.zeros((tokens, WIDTH), F32)
    for part in range(4):
        columns = slice(part * WIDTH, (part + 1) * WIDTH)
        before_grad = (joined_grad[part].astype(F32) * slope_ref[:, columns]).astype(BF16)
        normed_grad += dot_nt(before_grad, joined_here[part][...])
    grad = normalize_grad(rounded(normed_grad), normed, scale) + result_grad.astype(F32)
    grad = grad.astype(BF16)
    spread_grad = dot_nt(grad, lift_here[...])
    narrow_part = jnp.where(iota((tokens, LANES), 1) < 64, spread_grad[:, 384:], 0.0)
    left = jnp.where(
        kind == 2, spread_grad[:, :LANES], jnp.where(kind == 1, spread_grad[:, 256:384], narrow_part)
    )
    right = jnp.where(kind == 2, spread_grad[:, LANES:256], 0.0)
    row_grad = jnp.concatenate([left, right], axis=1).astype(BF16)
    term = dot_tn(spread, grad).reshape(devices // 2, CAP, WIDTH)
    term = jnp.stack([term[:, :, :256], term[:, :, 256:]], axis=1).reshape(devices, CAP, 256)
    placed = dot(placing, row_grad).reshape(devices, CAP, 256)
    payload_ref[...] = jnp.concatenate([placed, term], axis=1).astype(BF16)


def sum_kernel(landed_ref, share_ref):
    total = jnp.sum(landed_ref[...].astype(F32), axis=0)[CAP:]
    share_ref[...] = jnp.broadcast_to(total[None].astype(BF16), share_ref.shape)


def scatter_kernel(landed_ref, asked_ref, marks_ref, narrow_ref, middle_ref, wide_ref):
    sources = landed_ref.shape[0]
    amount = sources * CAP
    grads = landed_ref[...].astype(F32)[:, :CAP, :].reshape(amount, 256)
    code = request_codes(asked_ref, marks_ref[...])
    kind = code >> 11
    slab = code & 2047
    line = to_row(jnp.where(kind == 0, slab >> 1, slab))
    wide = jnp.where(kind == 2, grads, 0.0).astype(BF16)
    middle = jnp.where(kind == 1, grads[:, :LANES], 0.0).astype(BF16)
    narrow = jnp.where((kind == 0) & (iota((amount, LANES), 1) < 64), grads[:, :LANES], 0.0)
    narrow = jnp.where((slab & 1) == 1, pltpu.roll(narrow, 64, 1), narrow).astype(BF16)
    step = 256
    for start in range(0, wide_ref.shape[0], step):
        hot = one_hot(iota((step, amount), 0) + start == line)
        wide_ref[start : start + step, :] = dot(hot, wide)
        middle_ref[start : start + step, :] = dot(hot, middle)
        if start < narrow_ref.shape[0]:
            narrow_ref[start : start + step, :] = dot(hot, narrow)


def finish_kernel(
    rank_ref, list_ref, kept_ref, arrived_ref, shares_ref, output_ref, narrow_ref, middle_ref, wide_ref
):
    traded = traded_slot(rank_ref, list_ref)
    output_ref[1 - traded] = kept_ref[...]
    output_ref[traded] = arrived_ref[...]
    devices = shares_ref.shape[0]
    shares = shares_ref[...].astype(F32).reshape(devices // 2, 2, CAP, 256)
    for half in range(2):
        columns = slice(half * 256, (half + 1) * 256)
        whole = shares[:, half].reshape(devices // 2 * CAP, 256)
        wide_ref[:, columns] = whole[:256]
        middle_ref[:, columns] = whole[256:384]
        narrow_ref[:, columns] = whole[384:448]


SMEM = pl.BlockSpec(memory_space=pltpu.SMEM)
VMEM = pl.BlockSpec(memory_space=pltpu.VMEM)
HBM = pl.BlockSpec(memory_space=pltpu.HBM)
KEPT = pl.BlockSpec(memory_space=pltpu.VMEM)


def call(kernel, outs, args, scratch=(), flops=0, limit=LIMIT):
    arrays = []
    for space, array in args:
        if space is KEPT:
            array = pltpu.with_memory_space_constraint(array, pltpu.VMEM)
        elif space is not VMEM:
            array = pltpu.with_memory_space_constraint(array, pltpu.HBM)
        arrays.append(array)
    shapes = [
        pltpu.VMEM(out[0], out[1]) if KEPT in out[2:] else jax.ShapeDtypeStruct(out[0], out[1]) for out in outs
    ]
    moved = sum(a.size * a.dtype.itemsize for _, a in args)
    return pl.pallas_call(
        kernel,
        out_shape=shapes,
        in_specs=[space for space, _ in args],
        out_specs=[VMEM] * len(shapes),
        scratch_shapes=list(scratch),
        cost_estimate=pl.CostEstimate(flops=flops, bytes_accessed=moved, transcendentals=0),
        compiler_params=pltpu.CompilerParams(vmem_limit_bytes=int(limit * 2**20)),
    )(*arrays)


def exchange(array):
    return lax.all_to_all(array, ("dp", "table"), split_axis=0, concat_axis=0, tiled=True)


def body(
    history_lengths,
    balance_list,
    owner_device,
    owner_row,
    width_class,
    slab_index,
    narrow_table,
    middle_table,
    wide_table,
    narrow_lift,
    middle_lift,
    wide_lift,
    joined_weight,
    output_weight,
    cotangent,
):
    data_size = lax.axis_size("dp")
    table_size = lax.axis_size("table")
    devices = data_size * table_size
    rows = cotangent.shape[1]
    amount = devices * CAP
    data_rank = lax.axis_index("dp")
    self_rank = data_rank * table_size + lax.axis_index("table")
    rank = (SMEM, jnp.stack([data_rank, self_rank]).astype(I32))
    plan = (SMEM, balance_list.T)
    owner = owner_device.transpose(0, 2, 1)
    class_list = width_class.reshape(-1, LANES)
    partners = [(i, i ^ (data_size // 2)) for i in range(data_size)]

    requests, slots = call(
        request_kernel,
        [((devices, CAP), I32), (owner_row.shape, I32)],
        [(VMEM, owner), (VMEM, owner_row)],
        flops=10**8,
        limit=62,
    )
    asked = exchange(requests)
    slab_list = slab_index.reshape(-1, LANES)
    ready_cotangent, slots = lax.optimization_barrier((cotangent, slots))
    arrived_cotangent = lax.ppermute(ready_cotangent, "dp", partners)
    table, marks = call(
        stage_rows_kernel,
        [((middle_table.shape[0], 512), BF16, KEPT), ((slab_list.shape[0], 256), BF16, KEPT)],
        [
            rank, (HBM, slots), (HBM, class_list), (HBM, slab_list),
            (HBM, narrow_table), (HBM, middle_table), (HBM, wide_table),
        ],
        scratch=[
            pltpu.VMEM(slab_list.shape, I32), pltpu.VMEM(slab_list.shape, I32), pltpu.SemaphoreType.DMA((5,)),
        ],
    )
    (replies,) = call(
        owner_kernel,
        [((amount, 256), BF16)],
        [(VMEM, asked), (KEPT, marks), (KEPT, table)],
        flops=3 * 10**9,
    )
    replies, arrived_cotangent = lax.optimization_barrier((replies, arrived_cotangent))
    landed = exchange(replies)
    (kinds,) = call(
        class_kernel,
        [(owner_row.shape, I32)],
        [(VMEM, owner), (VMEM, owner_row), (HBM, class_list)],
        scratch=[pltpu.VMEM(class_list.shape, I32), pltpu.SemaphoreType.DMA],
        flops=10**9,
    )
    staged = call(
        stage_layer_kernel,
        [((WIDTH, WIDTH), BF16, KEPT)] * 3,
        [(HBM, slots), (HBM, narrow_lift), (HBM, middle_lift), (HBM, wide_lift), (HBM, joined_weight)],
        scratch=[pltpu.SemaphoreType.DMA((5,))],
    )
    kept_output, given_output, payload = call(
        layer_kernel,
        [((rows, WIDTH), BF16), ((rows, WIDTH), BF16), ((devices, 2 * CAP, 256), BF16)],
        [rank, plan, (SMEM, history_lengths.T), (VMEM, slots), (VMEM, landed), (VMEM, kinds)]
        + [(KEPT, array) for array in staged]
        + [(HBM, cotangent), (VMEM, arrived_cotangent), (HBM, joined_weight), (HBM, output_weight)],
        scratch=[
            pltpu.VMEM((WIDTH, WIDTH), BF16),
            pltpu.VMEM((WIDTH, WIDTH), BF16),
            pltpu.VMEM((WIDTH, WIDTH), BF16),
            pltpu.VMEM((2, rows, WIDTH), BF16),
            pltpu.VMEM((2 * rows, 4 * WIDTH), F32),
            pltpu.VMEM((2, HEADS, rows, rows), F32),
            pltpu.SemaphoreType.DMA((5,)),
        ],
        flops=10**10,
    )
    home = exchange(payload)
    (share,) = call(sum_kernel, [((devices, CAP, 256), BF16)], [(VMEM, home)])
    shares = exchange(share)
    given_output, _ = lax.optimization_barrier((given_output, share))
    arrived_output = lax.ppermute(given_output, "dp", partners)
    narrow_grad, middle_grad, wide_grad = call(
        scatter_kernel,
        [(narrow_table.shape, F32), (middle_table.shape, F32), (wide_table.shape, F32)],
        [(VMEM, home), (VMEM, asked), (KEPT, marks)],
        flops=3 * 10**9,
    )
    output, narrow_delta, middle_delta, wide_delta = call(
        finish_kernel,
        [
            (cotangent.shape, BF16), (narrow_lift.shape, F32), (middle_lift.shape, F32), (wide_lift.shape, F32),
        ],
        [rank, plan, (VMEM, kept_output), (VMEM, arrived_output), (VMEM, shares)],
    )
    return (output, narrow_grad, middle_grad, wide_grad, narrow_delta, middle_delta, wide_delta)


def solution(mesh):
    in_specs = (
        P(None, "table"),
        P(None, "table"),
        P(("dp", "table"), None, None),
        P(("dp", "table"), None),
        P(),
        P(("dp", "table")),
        P(("dp", "table"), None),
        P(("dp", "table"), None),
        P(("dp", "table"), None),
        P(),
        P(),
        P(),
        P(),
        P(),
        P(("dp", "table"), None, None),
    )
    out_specs = (
        P(("dp", "table"), None, None),
        P(("dp", "table"), None),
        P(("dp", "table"), None),
        P(("dp", "table"), None),
        P(),
        P(),
        P(),
    )
    return jax.shard_map(body, mesh=mesh, in_specs=in_specs, out_specs=out_specs, check_vma=False)
```

```python
import jax
import jax.numpy as jnp
from jax import lax
from jax.experimental import pallas as pl
from jax.experimental.pallas import tpu as pltpu
from jax.sharding import PartitionSpec as P

HEADS = 4
HEAD = 128
MAXLEN = 256
WIDTH = 512
CAP = 8
LANES = 128
OWNER_STEP = 256
LIMIT = 32

F32 = jnp.float32
BF16 = jnp.bfloat16
I32 = jnp.int32


def iota(shape, dim):
    return lax.broadcasted_iota(I32, shape, dim)


def one_hot(mask):
    return jnp.where(mask, 1.0, 0.0).astype(BF16)


def dot(a, b):
    return jnp.dot(a, b, preferred_element_type=F32)


def dot_nt(a, b):
    return lax.dot_general(a, b, (((1,), (1,)), ((), ())), preferred_element_type=F32)


def dot_tn(a, b):
    return lax.dot_general(a, b, (((0,), (0,)), ((), ())), preferred_element_type=F32)


def to_column(row):
    eye = iota((LANES, LANES), 0) == iota((LANES, LANES), 1)
    parts = []
    for start in range(0, row.shape[1], LANES):
        piece = row[:, start : start + LANES].astype(F32)
        parts.append(jnp.sum(jnp.where(eye, piece, 0.0), axis=1, keepdims=True))
    return jnp.concatenate(parts, axis=0).astype(I32)


def to_row(column):
    eye = iota((LANES, LANES), 0) == iota((LANES, LANES), 1)
    parts = []
    for start in range(0, column.shape[0], LANES):
        piece = column[start : start + LANES].astype(F32)
        parts.append(jnp.sum(jnp.where(eye, piece, 0.0), axis=0, keepdims=True))
    return jnp.concatenate(parts, axis=1).astype(I32)


def lane_sum(mask, values):
    return jnp.sum(jnp.where(mask, values, 0.0), axis=1, keepdims=True).astype(I32)


def flat_row(ref):
    return jnp.concatenate([ref[0:1, :], ref[1:2, :]], axis=1)


def request_kernel(owner_ref, item_ref, request_ref, slot_ref):
    devices = request_ref.shape[0]
    owner = jnp.concatenate([owner_ref[0], owner_ref[1]], axis=1)
    item = flat_row(item_ref)
    tokens = owner.shape[1]
    named = iota((devices, tokens), 0) == owner
    hot = one_hot(named)
    earlier = one_hot(iota((tokens, tokens), 0) < iota((tokens, tokens), 1))
    before = dot(hot, earlier)
    rank = jnp.sum(jnp.where(named, before, 0.0), axis=0, keepdims=True).astype(I32)
    place = iota((2 * CAP, tokens), 0)
    value = jnp.where(place < CAP, item >> 6, item & 63)
    table = jnp.where((place & (CAP - 1)) == rank, value, 0).astype(F32).astype(BF16)
    filled = dot_nt(hot, table).astype(I32)
    request_ref[...] = filled[:, :CAP] * 64 + filled[:, CAP:]
    slot = owner * CAP + rank
    half = tokens // 2
    slot_ref[0:1, :] = slot[:, :half]
    slot_ref[1:2, :] = slot[:, half:]


def class_kernel(owner_ref, item_ref, class_list_ref, class_ref, list_here, copied):
    copy = pltpu.make_async_copy(class_list_ref, list_here, copied)
    copy.start()
    item = to_column(flat_row(item_ref))
    owner = jnp.concatenate([owner_ref[0], owner_ref[1]], axis=1)
    line = to_column(owner) * (4096 // LANES) + (item >> 7)
    tokens = line.shape[0]
    lines = class_list_ref.shape[0]
    step = 512
    total = jnp.zeros((tokens, LANES), F32)
    copy.wait()
    for start in range(0, lines, step):
        hot = one_hot(iota((tokens, step), 1) + start == line)
        total += dot(hot, list_here[start : start + step, :].astype(F32).astype(BF16))
    kind = to_row(lane_sum(iota((tokens, LANES), 1) == (item & 127), total))
    class_ref[0:1, :] = kind[:, : tokens // 2]
    class_ref[1:2, :] = kind[:, tokens // 2 :]


def request_codes(asked_ref, marks):
    asked = asked_ref[...]
    sources = asked.shape[0]
    amount = sources * CAP
    expand = one_hot((iota((amount, sources), 0) >> 3) == iota((amount, sources), 1))
    mine = (iota((amount, CAP), 0) & (CAP - 1)) == iota((amount, CAP), 1)
    high = lane_sum(mine, dot(expand, (asked >> 7).astype(F32).astype(BF16)))
    low = lane_sum(mine, dot(expand, (asked & 127).astype(F32).astype(BF16)))
    found = dot(one_hot(iota((amount, marks.shape[0]), 1) == high), marks)
    mine = iota((amount, LANES), 1) == low
    return lane_sum(mine, found[:, LANES:]) * LANES + lane_sum(mine, found[:, :LANES])


def stage_rows_kernel(
    rank_ref, after_ref, class_list_ref, slab_ref, narrow_ref, middle_ref, wide_ref, table_ref, marks_ref,
    class_here, slab_here, copied,
):
    del after_ref
    groups = slab_here.shape[0]
    lines = narrow_ref.shape[0]
    moves = [
        (class_list_ref.at[pl.ds(pl.multiple_of(rank_ref[1] * groups, groups), groups)], class_here),
        (slab_ref, slab_here),
        (wide_ref, table_ref.at[:, 0:256]),
        (middle_ref, table_ref.at[:, 256:384]),
        (narrow_ref, table_ref.at[0:lines, 384:512]),
    ]
    copies = [pltpu.make_async_copy(there, here, copied.at[k]) for k, (there, here) in enumerate(moves)]
    for copy in copies:
        copy.start()
    table_ref[lines:, 384:] = jnp.zeros((table_ref.shape[0] - lines, LANES), BF16)
    for copy in copies:
        copy.wait()
    slab = slab_here[...]
    marks = jnp.concatenate([slab & 127, (slab >> 7) + 16 * class_here[...]], axis=1)
    marks_ref[...] = marks.astype(F32).astype(BF16)


def owner_kernel(asked_ref, marks_ref, table_ref, reply_ref):
    amount = reply_ref.shape[0]
    code = request_codes(asked_ref, marks_ref[...])
    kind = code >> 11
    slab = code & 2047
    line = jnp.where(kind == 0, slab >> 1, slab)
    lines = table_ref.shape[0]
    for start in range(0, amount, OWNER_STEP):
        rows = slice(start, start + OWNER_STEP)
        hot = one_hot(iota((OWNER_STEP, lines), 1) == line[rows])
        here = kind[rows]
        side = dot(hot, table_ref[:, 256:])
        narrow = side[:, LANES:]
        narrow = jnp.where((slab[rows] & 1) == 1, pltpu.roll(narrow, 64, 1), narrow)
        narrow = jnp.where(iota((OWNER_STEP, LANES), 1) < 64, narrow, 0.0)
        side = jnp.where(here == 1, side[:, :LANES], narrow)
        wide = dot(hot, table_ref[:, :256])
        left = jnp.where(here == 2, wide[:, :LANES], side)
        right = jnp.where(here == 2, wide[:, LANES:], 0.0)
        reply_ref[rows, :] = jnp.concatenate([left, right], axis=1).astype(BF16)


def traded_slot(rank_ref, list_ref):
    rank = rank_ref[0]
    return jnp.where((list_ref[0, rank] >> 1) != rank, 0, 1)


def stage_layer_kernel(
    rank_ref, list_ref, length_ref, after_ref, narrow_ref, middle_ref, wide_ref, joined_ref,
    facts_ref, lift_here, gating_here, values_here, copied,
):
    del after_ref
    rank = rank_ref[0]
    traded = traded_slot(rank_ref, list_ref)
    facts = [traded, list_ref[traded, rank] & 1, length_ref[0, rank], length_ref[1, rank]]
    for row, fact in enumerate(facts):
        facts_ref[row : row + 1, :] = jnp.full((1, LANES), fact, I32)
    moves = [
        (wide_ref, lift_here.at[0:256]),
        (middle_ref, lift_here.at[256:384]),
        (narrow_ref, lift_here.at[384:448]),
    ]
    for part, here in enumerate([gating_here, values_here]):
        moves.append((joined_ref.at[:, part * WIDTH : (part + 1) * WIDTH], here))
    copies = [pltpu.make_async_copy(there, here, copied.at[k]) for k, (there, here) in enumerate(moves)]
    for copy in copies:
        copy.start()
    lift_here[448:, :] = jnp.zeros((64, WIDTH), BF16)
    for copy in copies:
        copy.wait()


def mean(values):
    return jnp.sum(values, axis=1, keepdims=True) * (1.0 / WIDTH)


def normalize(values):
    centre = values - mean(values)
    scale = lax.rsqrt(mean(centre * centre) + 1e-06)
    return centre * scale, scale


def normalize_grad(grad, normed, scale):
    return scale * (grad - mean(grad) - normed * mean(grad * normed))


def sigmoid(values):
    return 0.5 * jnp.tanh(0.5 * values) + 0.5


def rounded(values):
    return values.astype(BF16).astype(F32)


def layer_kernel(
    facts_ref, slot_ref, landed_ref, class_ref, lift_here, gating_here, values_here,
    cotangent_ref, arrived_ref, joined_ref, output_weight_ref, kept_ref, given_ref, payload_ref,
    queries_here, keys_here, output_here, cotangent_here, slope_ref, curve_ref, copied,
):
    moves = [
        (joined_ref.at[:, 2 * WIDTH : 3 * WIDTH], queries_here),
        (joined_ref.at[:, 3 * WIDTH :], keys_here),
        (output_weight_ref, output_here),
        (cotangent_ref, cotangent_here),
    ]
    copies = [pltpu.make_async_copy(there, here, copied.at[k]) for k, (there, here) in enumerate(moves)]
    for copy in copies:
        copy.start()
    zero = jnp.zeros((), BF16)
    rows = kept_ref.shape[0]
    hists = slot_ref.shape[0]
    tokens = hists * rows
    devices = payload_ref.shape[0]
    amount = devices * CAP
    slot = flat_row(slot_ref)
    placing = one_hot(iota((amount, tokens), 0) == slot)
    raw = dot_tn(placing, landed_ref[...]).astype(BF16)
    kind = to_column(flat_row(class_ref))
    spread = jnp.concatenate(
        [
            jnp.where(kind == 2, raw, zero),
            jnp.where(kind == 1, raw[:, :LANES], zero),
            jnp.where(kind == 0, raw[:, :LANES], zero),
        ],
        axis=1,
    )
    widened = rounded(dot(spread, lift_here[...]))
    normed, scale = normalize(widened)
    normed_low = normed.astype(BF16)
    for copy in copies:
        copy.wait()
    joined_here = [gating_here, values_here, queries_here, keys_here]
    joined = []
    for part in range(4):
        columns = slice(part * WIDTH, (part + 1) * WIDTH)
        before = dot(normed_low, joined_here[part][...])
        gate = sigmoid(before)
        active = before * gate
        joined.append(active.astype(BF16))
        slope_ref[:, columns] = gate + active * (1.0 - gate)
    gating, values, queries, keys = joined
    gating = gating.astype(F32)
    place = iota((tokens, 1), 0)
    lengths = [facts_ref[2 + hist : 3 + hist, 0:1] for hist in range(hists)]
    traded = jnp.broadcast_to(facts_ref[0:1, 0:1], (rows, 1))
    source = jnp.broadcast_to(facts_ref[1:2, 0:1], (rows, 1))
    valid = place < jnp.where(place < rows, lengths[0], rows + lengths[1])
    across = iota((rows, rows), 1)
    causal = across <= iota((rows, rows), 0)
    weights = {}
    mixed = []
    for hist in range(hists):
        lines = slice(hist * rows, (hist + 1) * rows)
        factor = jnp.where(causal & (across < lengths[hist]), 1.0 / MAXLEN, 0.0)
        heads = []
        for head in range(HEADS):
            columns = slice(head * HEAD, (head + 1) * HEAD)
            scores = dot_nt(queries[lines, columns], keys[lines, columns])
            gate = sigmoid(scores)
            scaled = gate * factor
            active = scores * scaled
            weights[hist, head] = active.astype(BF16)
            curve_ref[hist, head] = scaled + active * (1.0 - gate)
            heads.append(dot(weights[hist, head], values[lines, columns]))
        mixed.append(jnp.concatenate(heads, axis=1))
    mixed_normed, mixed_scale = normalize(jnp.concatenate(mixed, axis=0))
    gated = (mixed_normed * gating).astype(BF16)
    result = dot(gated, output_here[...]) + widened
    output = jnp.where(valid, result, 0.0).astype(BF16)
    kept_ref[...] = jnp.where(traded == 0, output[rows:], output[:rows])
    given_ref[...] = jnp.where(traded == 0, output[:rows], output[rows:])

    came = jnp.where(source == 0, arrived_ref[0], arrived_ref[1])
    cotangent = jnp.concatenate(
        [jnp.where(traded == 0, came, cotangent_here[0]), jnp.where(traded == 0, cotangent_here[1], came)], axis=0
    )
    result_grad = jnp.where(valid, cotangent, zero)
    gated_grad = rounded(dot_nt(result_grad, output_here[...]))
    gating_grad = (gated_grad * mixed_normed).astype(BF16)
    mixed_grad = normalize_grad(gated_grad * gating, mixed_normed, mixed_scale).astype(BF16)
    grads = [[], [], []]
    for hist in range(hists):
        lines = slice(hist * rows, (hist + 1) * rows)
        heads = [[], [], []]
        for head in range(HEADS):
            columns = slice(head * HEAD, (head + 1) * HEAD)
            own = mixed_grad[lines, columns]
            weights_grad = rounded(dot_nt(own, values[lines, columns]))
            scores_grad = (weights_grad * curve_ref[hist, head]).astype(BF16)
            heads[0].append(dot_tn(weights[hist, head], own))
            heads[1].append(dot(scores_grad, keys[lines, columns]))
            heads[2].append(dot_tn(scores_grad, queries[lines, columns]))
        for part in range(3):
            grads[part].append(jnp.concatenate(heads[part], axis=1).astype(BF16))
    joined_grad = [gating_grad] + [jnp.concatenate(g, axis=0) for g in grads]
    normed_grad = jnp.zeros((tokens, WIDTH), F32)
    for part in range(4):
        columns = slice(part * WIDTH, (part + 1) * WIDTH)
        before_grad = (joined_grad[part].astype(F32) * slope_ref[:, columns]).astype(BF16)
        normed_grad += dot_nt(before_grad, joined_here[part][...])
    grad = normalize_grad(rounded(normed_grad), normed, scale) + result_grad.astype(F32)
    grad = grad.astype(BF16)
    spread_grad = dot_nt(grad, lift_here[...])
    narrow_part = jnp.where(iota((tokens, LANES), 1) < 64, spread_grad[:, 384:], 0.0)
    left = jnp.where(
        kind == 2, spread_grad[:, :LANES], jnp.where(kind == 1, spread_grad[:, 256:384], narrow_part)
    )
    right = jnp.where(kind == 2, spread_grad[:, LANES:256], 0.0)
    row_grad = jnp.concatenate([left, right], axis=1).astype(BF16)
    term = dot_tn(spread, grad).reshape(devices // 2, CAP, WIDTH)
    term = jnp.stack([term[:, :, :256], term[:, :, 256:]], axis=1).reshape(devices, CAP, 256)
    placed = dot(placing, row_grad).reshape(devices, CAP, 256)
    payload_ref[...] = jnp.concatenate([placed, term], axis=1).astype(BF16)


def sum_kernel(landed_ref, share_ref):
    total = jnp.sum(landed_ref[...].astype(F32), axis=0)[CAP:]
    share_ref[...] = jnp.broadcast_to(total[None].astype(BF16), share_ref.shape)


def scatter_kernel(landed_ref, asked_ref, marks_ref, narrow_ref, middle_ref, wide_ref):
    sources = landed_ref.shape[0]
    amount = sources * CAP
    grads = landed_ref[...].astype(F32)[:, :CAP, :].reshape(amount, 256)
    code = request_codes(asked_ref, marks_ref[...])
    kind = code >> 11
    slab = code & 2047
    line = to_row(jnp.where(kind == 0, slab >> 1, slab))
    wide = jnp.where(kind == 2, grads, 0.0).astype(BF16)
    middle = jnp.where(kind == 1, grads[:, :LANES], 0.0).astype(BF16)
    narrow = jnp.where((kind == 0) & (iota((amount, LANES), 1) < 64), grads[:, :LANES], 0.0)
    narrow = jnp.where((slab & 1) == 1, pltpu.roll(narrow, 64, 1), narrow).astype(BF16)
    step = 256
    for start in range(0, wide_ref.shape[0], step):
        hot = one_hot(iota((step, amount), 0) + start == line)
        wide_ref[start : start + step, :] = dot(hot, wide)
        middle_ref[start : start + step, :] = dot(hot, middle)
        if start < narrow_ref.shape[0]:
            narrow_ref[start : start + step, :] = dot(hot, narrow)


def finish_kernel(
    facts_ref, kept_ref, arrived_ref, shares_ref, output_ref, narrow_ref, middle_ref, wide_ref
):
    traded = jnp.broadcast_to(facts_ref[0:1, 0:1], (kept_ref.shape[0], 1))
    kept = kept_ref[...]
    arrived = arrived_ref[...]
    output_ref[0] = jnp.where(traded == 0, arrived, kept)
    output_ref[1] = jnp.where(traded == 0, kept, arrived)
    devices = shares_ref.shape[0]
    shares = shares_ref[...].astype(F32).reshape(devices // 2, 2, CAP, 256)
    for half in range(2):
        columns = slice(half * 256, (half + 1) * 256)
        whole = shares[:, half].reshape(devices // 2 * CAP, 256)
        wide_ref[:, columns] = whole[:256]
        middle_ref[:, columns] = whole[256:384]
        narrow_ref[:, columns] = whole[384:448]


SMEM = pl.BlockSpec(memory_space=pltpu.SMEM)
VMEM = pl.BlockSpec(memory_space=pltpu.VMEM)
HBM = pl.BlockSpec(memory_space=pltpu.HBM)
KEPT = pl.BlockSpec(memory_space=pltpu.VMEM)


def call(kernel, outs, args, scratch=(), flops=0, limit=LIMIT):
    arrays = []
    for space, array in args:
        if space is KEPT:
            array = pltpu.with_memory_space_constraint(array, pltpu.VMEM)
        elif space is not VMEM:
            array = pltpu.with_memory_space_constraint(array, pltpu.HBM)
        arrays.append(array)
    shapes = [
        pltpu.VMEM(out[0], out[1]) if KEPT in out[2:] else jax.ShapeDtypeStruct(out[0], out[1]) for out in outs
    ]
    moved = sum(a.size * a.dtype.itemsize for _, a in args)
    return pl.pallas_call(
        kernel,
        out_shape=shapes,
        in_specs=[space for space, _ in args],
        out_specs=[VMEM] * len(shapes),
        scratch_shapes=list(scratch),
        cost_estimate=pl.CostEstimate(flops=flops, bytes_accessed=moved, transcendentals=0),
        compiler_params=pltpu.CompilerParams(vmem_limit_bytes=int(limit * 2**20)),
    )(*arrays)


def exchange(array):
    return lax.all_to_all(array, ("dp", "table"), split_axis=0, concat_axis=0, tiled=True)


def body(
    history_lengths,
    balance_list,
    owner_device,
    owner_row,
    width_class,
    slab_index,
    narrow_table,
    middle_table,
    wide_table,
    narrow_lift,
    middle_lift,
    wide_lift,
    joined_weight,
    output_weight,
    cotangent,
):
    data_size = lax.axis_size("dp")
    table_size = lax.axis_size("table")
    devices = data_size * table_size
    rows = cotangent.shape[1]
    amount = devices * CAP
    data_rank = lax.axis_index("dp")
    self_rank = data_rank * table_size + lax.axis_index("table")
    rank = (SMEM, jnp.stack([data_rank, self_rank]).astype(I32))
    plan = (SMEM, balance_list.T)
    owner = owner_device.transpose(0, 2, 1)
    class_list = width_class.reshape(-1, LANES)
    partners = [(i, i ^ (data_size // 2)) for i in range(data_size)]

    requests, slots = call(
        request_kernel,
        [((devices, CAP), I32), (owner_row.shape, I32)],
        [(VMEM, owner), (VMEM, owner_row)],
        flops=10**8,
        limit=62,
    )
    asked = exchange(requests)
    slab_list = slab_index.reshape(-1, LANES)
    ready_cotangent, slots = lax.optimization_barrier((cotangent, slots))
    arrived_cotangent = lax.ppermute(ready_cotangent, "dp", partners)
    table, marks = call(
        stage_rows_kernel,
        [((middle_table.shape[0], 512), BF16, KEPT), ((slab_list.shape[0], 256), BF16, KEPT)],
        [
            rank, (HBM, slots), (HBM, class_list), (HBM, slab_list),
            (HBM, narrow_table), (HBM, middle_table), (HBM, wide_table),
        ],
        scratch=[
            pltpu.VMEM(slab_list.shape, I32), pltpu.VMEM(slab_list.shape, I32), pltpu.SemaphoreType.DMA((5,)),
        ],
    )
    (replies,) = call(
        owner_kernel,
        [((amount, 256), BF16)],
        [(VMEM, asked), (KEPT, marks), (KEPT, table)],
        flops=3 * 10**9,
    )
    replies, arrived_cotangent = lax.optimization_barrier((replies, arrived_cotangent))
    landed = exchange(replies)
    (kinds,) = call(
        class_kernel,
        [(owner_row.shape, I32)],
        [(VMEM, owner), (VMEM, owner_row), (HBM, class_list)],
        scratch=[pltpu.VMEM(class_list.shape, I32), pltpu.SemaphoreType.DMA],
        flops=10**9,
    )
    facts, *staged = call(
        stage_layer_kernel,
        [((8, LANES), I32, KEPT)] + [((WIDTH, WIDTH), BF16, KEPT)] * 3,
        [rank, plan, (SMEM, history_lengths.T), (HBM, slots), (HBM, narrow_lift), (HBM, middle_lift), (HBM, wide_lift), (HBM, joined_weight)],
        scratch=[pltpu.SemaphoreType.DMA((5,))],
    )
    kept_output, given_output, payload = call(
        layer_kernel,
        [((rows, WIDTH), BF16), ((rows, WIDTH), BF16), ((devices, 2 * CAP, 256), BF16)],
        [(KEPT, facts), (VMEM, slots), (VMEM, landed), (VMEM, kinds)]
        + [(KEPT, array) for array in staged]
        + [(HBM, cotangent), (VMEM, arrived_cotangent), (HBM, joined_weight), (HBM, output_weight)],
        scratch=[
            pltpu.VMEM((WIDTH, WIDTH), BF16),
            pltpu.VMEM((WIDTH, WIDTH), BF16),
            pltpu.VMEM((WIDTH, WIDTH), BF16),
            pltpu.VMEM((2, rows, WIDTH), BF16),
            pltpu.VMEM((2 * rows, 4 * WIDTH), F32),
            pltpu.VMEM((2, HEADS, rows, rows), F32),
            pltpu.SemaphoreType.DMA((4,)),
        ],
        flops=10**10,
    )
    home = exchange(payload)
    (share,) = call(sum_kernel, [((devices, CAP, 256), BF16)], [(VMEM, home)])
    shares = exchange(share)
    given_output, _ = lax.optimization_barrier((given_output, share))
    arrived_output = lax.ppermute(given_output, "dp", partners)
    narrow_grad, middle_grad, wide_grad = call(
        scatter_kernel,
        [(narrow_table.shape, F32), (middle_table.shape, F32), (wide_table.shape, F32)],
        [(VMEM, home), (VMEM, asked), (KEPT, marks)],
        flops=3 * 10**9,
    )
    output, narrow_delta, middle_delta, wide_delta = call(
        finish_kernel,
        [
            (cotangent.shape, BF16), (narrow_lift.shape, F32), (middle_lift.shape, F32), (wide_lift.shape, F32),
        ],
        [(KEPT, facts), (VMEM, kept_output), (VMEM, arrived_output), (VMEM, shares)],
    )
    return (output, narrow_grad, middle_grad, wide_grad, narrow_delta, middle_delta, wide_delta)


def solution(mesh):
    in_specs = (
        P(None, "table"),
        P(None, "table"),
        P(("dp", "table"), None, None),
        P(("dp", "table"), None),
        P(),
        P(("dp", "table")),
        P(("dp", "table"), None),
        P(("dp", "table"), None),
        P(("dp", "table"), None),
        P(),
        P(),
        P(),
        P(),
        P(),
        P(("dp", "table"), None, None),
    )
    out_specs = (
        P(("dp", "table"), None, None),
        P(("dp", "table"), None),
        P(("dp", "table"), None),
        P(("dp", "table"), None),
        P(),
        P(),
        P(),
    )
    return jax.shard_map(body, mesh=mesh, in_specs=in_specs, out_specs=out_specs, check_vma=False)
```

```python
import jax
import jax.numpy as jnp
from jax import lax
from jax.experimental import pallas as pl
from jax.experimental.pallas import tpu as pltpu
from jax.sharding import PartitionSpec as P

HEADS = 4
HEAD = 128
MAXLEN = 256
WIDTH = 512
CAP = 8
LANES = 128
OWNER_STEP = 256
LIMIT = 32

F32 = jnp.float32
BF16 = jnp.bfloat16
I32 = jnp.int32


def iota(shape, dim):
    return lax.broadcasted_iota(I32, shape, dim)


def one_hot(mask):
    return jnp.where(mask, 1.0, 0.0).astype(BF16)


def dot(a, b):
    return jnp.dot(a, b, preferred_element_type=F32)


def dot_nt(a, b):
    return lax.dot_general(a, b, (((1,), (1,)), ((), ())), preferred_element_type=F32)


def dot_tn(a, b):
    return lax.dot_general(a, b, (((0,), (0,)), ((), ())), preferred_element_type=F32)


def to_column(row):
    eye = iota((LANES, LANES), 0) == iota((LANES, LANES), 1)
    parts = []
    for start in range(0, row.shape[1], LANES):
        piece = row[:, start : start + LANES].astype(F32)
        parts.append(jnp.sum(jnp.where(eye, piece, 0.0), axis=1, keepdims=True))
    return jnp.concatenate(parts, axis=0).astype(I32)


def to_row(column):
    eye = iota((LANES, LANES), 0) == iota((LANES, LANES), 1)
    parts = []
    for start in range(0, column.shape[0], LANES):
        piece = column[start : start + LANES].astype(F32)
        parts.append(jnp.sum(jnp.where(eye, piece, 0.0), axis=0, keepdims=True))
    return jnp.concatenate(parts, axis=1).astype(I32)


def lane_sum(mask, values):
    return jnp.sum(jnp.where(mask, values, 0.0), axis=1, keepdims=True).astype(I32)


def flat_row(ref):
    return jnp.concatenate([ref[0:1, :], ref[1:2, :]], axis=1)


def request_kernel(owner_ref, item_ref, request_ref, slot_ref):
    devices = request_ref.shape[0]
    owner = jnp.concatenate([owner_ref[0], owner_ref[1]], axis=1)
    item = flat_row(item_ref)
    tokens = owner.shape[1]
    named = iota((devices, tokens), 0) == owner
    hot = one_hot(named)
    earlier = one_hot(iota((tokens, tokens), 0) < iota((tokens, tokens), 1))
    before = dot(hot, earlier)
    rank = jnp.sum(jnp.where(named, before, 0.0), axis=0, keepdims=True).astype(I32)
    place = iota((2 * CAP, tokens), 0)
    value = jnp.where(place < CAP, item >> 6, item & 63)
    table = jnp.where((place & (CAP - 1)) == rank, value, 0).astype(F32).astype(BF16)
    filled = dot_nt(hot, table).astype(I32)
    request_ref[...] = filled[:, :CAP] * 64 + filled[:, CAP:]
    slot = owner * CAP + rank
    half = tokens // 2
    slot_ref[0:1, :] = slot[:, :half]
    slot_ref[1:2, :] = slot[:, half:]


def class_kernel(owner_ref, item_ref, class_list_ref, class_ref, list_here, copied):
    copy = pltpu.make_async_copy(class_list_ref, list_here, copied)
    copy.start()
    item = to_column(flat_row(item_ref))
    owner = jnp.concatenate([owner_ref[0], owner_ref[1]], axis=1)
    line = to_column(owner) * (4096 // LANES) + (item >> 7)
    tokens = line.shape[0]
    lines = class_list_ref.shape[0]
    step = 512
    total = jnp.zeros((tokens, LANES), F32)
    copy.wait()
    for start in range(0, lines, step):
        hot = one_hot(iota((tokens, step), 1) + start == line)
        total += dot(hot, list_here[start : start + step, :].astype(F32).astype(BF16))
    kind = to_row(lane_sum(iota((tokens, LANES), 1) == (item & 127), total))
    class_ref[0:1, :] = kind[:, : tokens // 2]
    class_ref[1:2, :] = kind[:, tokens // 2 :]


def request_codes(asked_ref, marks):
    asked = asked_ref[...]
    sources = asked.shape[0]
    amount = sources * CAP
    expand = one_hot((iota((amount, sources), 0) >> 3) == iota((amount, sources), 1))
    mine = (iota((amount, CAP), 0) & (CAP - 1)) == iota((amount, CAP), 1)
    high = lane_sum(mine, dot(expand, (asked >> 7).astype(F32).astype(BF16)))
    low = lane_sum(mine, dot(expand, (asked & 127).astype(F32).astype(BF16)))
    found = dot(one_hot(iota((amount, marks.shape[0]), 1) == high), marks)
    mine = iota((amount, LANES), 1) == low
    return lane_sum(mine, found[:, LANES:]) * LANES + lane_sum(mine, found[:, :LANES])


def stage_rows_kernel(
    rank_ref, after_ref, class_list_ref, slab_ref, narrow_ref, middle_ref, wide_ref, table_ref, marks_ref,
    class_here, slab_here, copied,
):
    del after_ref
    groups = slab_here.shape[0]
    lines = narrow_ref.shape[0]
    moves = [
        (class_list_ref.at[pl.ds(pl.multiple_of(rank_ref[1] * groups, groups), groups)], class_here),
        (slab_ref, slab_here),
        (wide_ref, table_ref.at[:, 0:256]),
        (middle_ref, table_ref.at[:, 256:384]),
        (narrow_ref, table_ref.at[0:lines, 384:512]),
    ]
    copies = [pltpu.make_async_copy(there, here, copied.at[k]) for k, (there, here) in enumerate(moves)]
    for copy in copies:
        copy.start()
    table_ref[lines:, 384:] = jnp.zeros((table_ref.shape[0] - lines, LANES), BF16)
    for copy in copies:
        copy.wait()
    slab = slab_here[...]
    marks = jnp.concatenate([slab & 127, (slab >> 7) + 16 * class_here[...]], axis=1)
    marks_ref[...] = marks.astype(F32).astype(BF16)


def owner_kernel(asked_ref, marks_ref, table_ref, reply_ref):
    amount = reply_ref.shape[0]
    code = request_codes(asked_ref, marks_ref[...])
    kind = code >> 11
    slab = code & 2047
    line = jnp.where(kind == 0, slab >> 1, slab)
    lines = table_ref.shape[0]
    for start in range(0, amount, OWNER_STEP):
        rows = slice(start, start + OWNER_STEP)
        hot = one_hot(iota((OWNER_STEP, lines), 1) == line[rows])
        here = kind[rows]
        side = dot(hot, table_ref[:, 256:])
        narrow = side[:, LANES:]
        narrow = jnp.where((slab[rows] & 1) == 1, pltpu.roll(narrow, 64, 1), narrow)
        narrow = jnp.where(iota((OWNER_STEP, LANES), 1) < 64, narrow, 0.0)
        side = jnp.where(here == 1, side[:, :LANES], narrow)
        wide = dot(hot, table_ref[:, :256])
        left = jnp.where(here == 2, wide[:, :LANES], side)
        right = jnp.where(here == 2, wide[:, LANES:], 0.0)
        reply_ref[rows, :] = jnp.concatenate([left, right], axis=1).astype(BF16)


def traded_slot(rank_ref, list_ref):
    rank = rank_ref[0]
    return jnp.where((list_ref[0, rank] >> 1) != rank, 0, 1)


def stage_layer_kernel(
    rank_ref, list_ref, length_ref, after_ref, narrow_ref, middle_ref, wide_ref, joined_ref,
    facts_ref, lift_here, gating_here, values_here, copied,
):
    del after_ref
    rank = rank_ref[0]
    traded = traded_slot(rank_ref, list_ref)
    facts = [traded, list_ref[traded, rank] & 1, length_ref[0, rank], length_ref[1, rank]]
    for row, fact in enumerate(facts):
        facts_ref[row : row + 1, :] = jnp.full((1, LANES), fact, I32)
    moves = [
        (wide_ref, lift_here.at[0:256]),
        (middle_ref, lift_here.at[256:384]),
        (narrow_ref, lift_here.at[384:448]),
    ]
    for part, here in enumerate([gating_here, values_here]):
        moves.append((joined_ref.at[:, part * WIDTH : (part + 1) * WIDTH], here))
    copies = [pltpu.make_async_copy(there, here, copied.at[k]) for k, (there, here) in enumerate(moves)]
    for copy in copies:
        copy.start()
    lift_here[448:, :] = jnp.zeros((64, WIDTH), BF16)
    for copy in copies:
        copy.wait()


def mean(values):
    return jnp.sum(values, axis=1, keepdims=True) * (1.0 / WIDTH)


def normalize(values):
    centre = values - mean(values)
    scale = lax.rsqrt(mean(centre * centre) + 1e-06)
    return centre * scale, scale


def normalize_grad(grad, normed, scale):
    return scale * (grad - mean(grad) - normed * mean(grad * normed))


def sigmoid(values):
    return 0.5 * jnp.tanh(0.5 * values) + 0.5


def rounded(values):
    return values.astype(BF16).astype(F32)


def layer_kernel(
    facts_ref, slot_ref, landed_ref, class_ref, lift_here, gating_here, values_here,
    cotangent_ref, arrived_ref, joined_ref, output_weight_ref, kept_ref, given_ref, payload_ref,
    queries_here, keys_here, output_here, cotangent_here, slope_ref, curve_ref, copied,
):
    moves = [
        (joined_ref.at[:, 2 * WIDTH : 3 * WIDTH], queries_here),
        (joined_ref.at[:, 3 * WIDTH :], keys_here),
        (output_weight_ref, output_here),
        (cotangent_ref, cotangent_here),
    ]
    copies = [pltpu.make_async_copy(there, here, copied.at[k]) for k, (there, here) in enumerate(moves)]
    for copy in copies:
        copy.start()
    zero = jnp.zeros((), BF16)
    rows = kept_ref.shape[0]
    hists = slot_ref.shape[0]
    tokens = hists * rows
    devices = payload_ref.shape[0]
    amount = devices * CAP
    slot = flat_row(slot_ref)
    placing = one_hot(iota((amount, tokens), 0) == slot)
    raw = dot_tn(placing, landed_ref[...]).astype(BF16)
    kind = to_column(flat_row(class_ref))
    spread = jnp.concatenate(
        [
            jnp.where(kind == 2, raw, zero),
            jnp.where(kind == 1, raw[:, :LANES], zero),
            jnp.where(kind == 0, raw[:, :LANES], zero),
        ],
        axis=1,
    )
    widened = rounded(dot(spread, lift_here[...]))
    normed, scale = normalize(widened)
    normed_low = normed.astype(BF16)
    for copy in copies:
        copy.wait()
    joined_here = [gating_here, values_here, queries_here, keys_here]
    joined = []
    for part in range(4):
        columns = slice(part * WIDTH, (part + 1) * WIDTH)
        before = dot(normed_low, joined_here[part][...])
        gate = sigmoid(before)
        active = before * gate
        joined.append(active.astype(BF16))
        slope_ref[:, columns] = gate + active * (1.0 - gate)
    gating, values, queries, keys = joined
    gating = gating.astype(F32)
    place = iota((tokens, 1), 0)
    lengths = [facts_ref[2 + hist : 3 + hist, 0:1] for hist in range(hists)]
    traded = jnp.broadcast_to(facts_ref[0:1, 0:1], (rows, 1))
    source = jnp.broadcast_to(facts_ref[1:2, 0:1], (rows, 1))
    valid = place < jnp.where(place < rows, lengths[0], rows + lengths[1])
    across = iota((rows, rows), 1)
    causal = across <= iota((rows, rows), 0)
    weights = {}
    mixed = []
    for hist in range(hists):
        lines = slice(hist * rows, (hist + 1) * rows)
        factor = jnp.where(causal & (across < lengths[hist]), 1.0 / MAXLEN, 0.0)
        heads = []
        for head in range(HEADS):
            columns = slice(head * HEAD, (head + 1) * HEAD)
            scores = dot_nt(queries[lines, columns], keys[lines, columns])
            gate = sigmoid(scores)
            scaled = gate * factor
            active = scores * scaled
            weights[hist, head] = active.astype(BF16)
            curve_ref[hist, head] = scaled + active * (1.0 - gate)
            heads.append(dot(weights[hist, head], values[lines, columns]))
        mixed.append(jnp.concatenate(heads, axis=1))
    mixed_normed, mixed_scale = normalize(jnp.concatenate(mixed, axis=0))
    gated = (mixed_normed * gating).astype(BF16)
    result = dot(gated, output_here[...]) + widened
    output = jnp.where(valid, result, 0.0).astype(BF16)
    kept_ref[...] = jnp.where(traded == 0, output[rows:], output[:rows])
    given_ref[...] = jnp.where(traded == 0, output[:rows], output[rows:])

    came = jnp.where(source == 0, arrived_ref[0], arrived_ref[1])
    cotangent = jnp.concatenate(
        [jnp.where(traded == 0, came, cotangent_here[0]), jnp.where(traded == 0, cotangent_here[1], came)], axis=0
    )
    result_grad = jnp.where(valid, cotangent, zero)
    gated_grad = rounded(dot_nt(result_grad, output_here[...]))
    gating_grad = (gated_grad * mixed_normed).astype(BF16)
    mixed_grad = normalize_grad(gated_grad * gating, mixed_normed, mixed_scale).astype(BF16)
    grads = [[], [], []]
    for hist in range(hists):
        lines = slice(hist * rows, (hist + 1) * rows)
        heads = [[], [], []]
        for head in range(HEADS):
            columns = slice(head * HEAD, (head + 1) * HEAD)
            own = mixed_grad[lines, columns]
            weights_grad = rounded(dot_nt(own, values[lines, columns]))
            scores_grad = (weights_grad * curve_ref[hist, head]).astype(BF16)
            heads[0].append(dot_tn(weights[hist, head], own))
            heads[1].append(dot(scores_grad, keys[lines, columns]))
            heads[2].append(dot_tn(scores_grad, queries[lines, columns]))
        for part in range(3):
            grads[part].append(jnp.concatenate(heads[part], axis=1).astype(BF16))
    joined_grad = [gating_grad] + [jnp.concatenate(g, axis=0) for g in grads]
    normed_grad = jnp.zeros((tokens, WIDTH), F32)
    for part in range(4):
        columns = slice(part * WIDTH, (part + 1) * WIDTH)
        before_grad = (joined_grad[part].astype(F32) * slope_ref[:, columns]).astype(BF16)
        normed_grad += dot_nt(before_grad, joined_here[part][...])
    grad = normalize_grad(rounded(normed_grad), normed, scale) + result_grad.astype(F32)
    grad = grad.astype(BF16)
    spread_grad = dot_nt(grad, lift_here[...])
    narrow_part = jnp.where(iota((tokens, LANES), 1) < 64, spread_grad[:, 384:], 0.0)
    left = jnp.where(
        kind == 2, spread_grad[:, :LANES], jnp.where(kind == 1, spread_grad[:, 256:384], narrow_part)
    )
    right = jnp.where(kind == 2, spread_grad[:, LANES:256], 0.0)
    row_grad = jnp.concatenate([left, right], axis=1).astype(BF16)
    term = dot_tn(spread, grad).reshape(devices // 2, CAP, WIDTH)
    term = jnp.stack([term[:, :, :256], term[:, :, 256:]], axis=1).reshape(devices, CAP, 256)
    placed = dot(placing, row_grad).reshape(devices, CAP, 256)
    payload_ref[...] = jnp.concatenate([placed, term], axis=1).astype(BF16)


def sum_kernel(landed_ref, share_ref):
    total = jnp.sum(landed_ref[...].astype(F32), axis=0)[CAP:]
    share_ref[...] = jnp.broadcast_to(total[None].astype(BF16), share_ref.shape)


def scatter_kernel(landed_ref, asked_ref, marks_ref, narrow_ref, middle_ref, wide_ref):
    sources = landed_ref.shape[0]
    amount = sources * CAP
    grads = landed_ref[...].astype(F32)[:, :CAP, :].reshape(amount, 256)
    code = request_codes(asked_ref, marks_ref[...])
    kind = code >> 11
    slab = code & 2047
    line = to_row(jnp.where(kind == 0, slab >> 1, slab))
    wide = jnp.where(kind == 2, grads, 0.0).astype(BF16)
    middle = jnp.where(kind == 1, grads[:, :LANES], 0.0).astype(BF16)
    narrow = jnp.where((kind == 0) & (iota((amount, LANES), 1) < 64), grads[:, :LANES], 0.0)
    narrow = jnp.where((slab & 1) == 1, pltpu.roll(narrow, 64, 1), narrow).astype(BF16)
    step = 256
    for start in range(0, wide_ref.shape[0], step):
        hot = one_hot(iota((step, amount), 0) + start == line)
        wide_ref[start : start + step, :] = dot(hot, wide)
        middle_ref[start : start + step, :] = dot(hot, middle)
        if start < narrow_ref.shape[0]:
            narrow_ref[start : start + step, :] = dot(hot, narrow)


def finish_kernel(
    facts_ref, kept_ref, arrived_ref, shares_ref, output_ref, narrow_ref, middle_ref, wide_ref
):
    traded = jnp.broadcast_to(facts_ref[0:1, 0:1], (kept_ref.shape[0], 1))
    kept = kept_ref[...]
    arrived = arrived_ref[...]
    output_ref[0] = jnp.where(traded == 0, arrived, kept)
    output_ref[1] = jnp.where(traded == 0, kept, arrived)
    devices = shares_ref.shape[0]
    shares = shares_ref[...].astype(F32).reshape(devices // 2, 2, CAP, 256)
    for half in range(2):
        columns = slice(half * 256, (half + 1) * 256)
        whole = shares[:, half].reshape(devices // 2 * CAP, 256)
        wide_ref[:, columns] = whole[:256]
        middle_ref[:, columns] = whole[256:384]
        narrow_ref[:, columns] = whole[384:448]


SMEM = pl.BlockSpec(memory_space=pltpu.SMEM)
VMEM = pl.BlockSpec(memory_space=pltpu.VMEM)
HBM = pl.BlockSpec(memory_space=pltpu.HBM)
KEPT = pl.BlockSpec(memory_space=pltpu.VMEM)


def call(kernel, outs, args, scratch=(), flops=0, limit=LIMIT):
    arrays = []
    for space, array in args:
        if space is KEPT:
            array = pltpu.with_memory_space_constraint(array, pltpu.VMEM)
        elif space is not VMEM:
            array = pltpu.with_memory_space_constraint(array, pltpu.HBM)
        arrays.append(array)
    shapes = [
        pltpu.VMEM(out[0], out[1]) if KEPT in out[2:] else jax.ShapeDtypeStruct(out[0], out[1]) for out in outs
    ]
    moved = sum(a.size * a.dtype.itemsize for _, a in args)
    return pl.pallas_call(
        kernel,
        out_shape=shapes,
        in_specs=[space for space, _ in args],
        out_specs=[VMEM] * len(shapes),
        scratch_shapes=list(scratch),
        cost_estimate=pl.CostEstimate(flops=flops, bytes_accessed=moved, transcendentals=0),
        compiler_params=pltpu.CompilerParams(vmem_limit_bytes=int(limit * 2**20)),
    )(*arrays)


def exchange(array):
    return lax.all_to_all(array, ("dp", "table"), split_axis=0, concat_axis=0, tiled=True)


def body(
    history_lengths,
    balance_list,
    owner_device,
    owner_row,
    width_class,
    slab_index,
    narrow_table,
    middle_table,
    wide_table,
    narrow_lift,
    middle_lift,
    wide_lift,
    joined_weight,
    output_weight,
    cotangent,
):
    data_size = lax.axis_size("dp")
    table_size = lax.axis_size("table")
    devices = data_size * table_size
    rows = cotangent.shape[1]
    amount = devices * CAP
    data_rank = lax.axis_index("dp")
    self_rank = data_rank * table_size + lax.axis_index("table")
    rank = (SMEM, jnp.stack([data_rank, self_rank]).astype(I32))
    plan = (SMEM, balance_list.T)
    owner = owner_device.transpose(0, 2, 1)
    class_list = width_class.reshape(-1, LANES)
    partners = [(i, i ^ (data_size // 2)) for i in range(data_size)]

    requests, slots = call(
        request_kernel,
        [((devices, CAP), I32), (owner_row.shape, I32)],
        [(VMEM, owner), (VMEM, owner_row)],
        flops=10**8,
        limit=62,
    )
    asked = exchange(requests)
    slab_list = slab_index.reshape(-1, LANES)
    arrived_cotangent = lax.ppermute(cotangent, "dp", partners)
    table, marks = call(
        stage_rows_kernel,
        [((middle_table.shape[0], 512), BF16, KEPT), ((slab_list.shape[0], 256), BF16, KEPT)],
        [
            rank, (HBM, slots), (HBM, class_list), (HBM, slab_list),
            (HBM, narrow_table), (HBM, middle_table), (HBM, wide_table),
        ],
        scratch=[
            pltpu.VMEM(slab_list.shape, I32), pltpu.VMEM(slab_list.shape, I32), pltpu.SemaphoreType.DMA((5,)),
        ],
    )
    (replies,) = call(
        owner_kernel,
        [((amount, 256), BF16)],
        [(VMEM, asked), (KEPT, marks), (KEPT, table)],
        flops=3 * 10**9,
    )
    replies, arrived_cotangent = lax.optimization_barrier((replies, arrived_cotangent))
    landed = exchange(replies)
    (kinds,) = call(
        class_kernel,
        [(owner_row.shape, I32)],
        [(VMEM, owner), (VMEM, owner_row), (HBM, class_list)],
        scratch=[pltpu.VMEM(class_list.shape, I32), pltpu.SemaphoreType.DMA],
        flops=10**9,
    )
    facts, *staged = call(
        stage_layer_kernel,
        [((8, LANES), I32, KEPT)] + [((WIDTH, WIDTH), BF16, KEPT)] * 3,
        [rank, plan, (SMEM, history_lengths.T), (HBM, slots), (HBM, narrow_lift), (HBM, middle_lift), (HBM, wide_lift), (HBM, joined_weight)],
        scratch=[pltpu.SemaphoreType.DMA((5,))],
    )
    kept_output, given_output, payload = call(
        layer_kernel,
        [((rows, WIDTH), BF16), ((rows, WIDTH), BF16), ((devices, 2 * CAP, 256), BF16)],
        [(KEPT, facts), (VMEM, slots), (VMEM, landed), (VMEM, kinds)]
        + [(KEPT, array) for array in staged]
        + [(HBM, cotangent), (VMEM, arrived_cotangent), (HBM, joined_weight), (HBM, output_weight)],
        scratch=[
            pltpu.VMEM((WIDTH, WIDTH), BF16),
            pltpu.VMEM((WIDTH, WIDTH), BF16),
            pltpu.VMEM((WIDTH, WIDTH), BF16),
            pltpu.VMEM((2, rows, WIDTH), BF16),
            pltpu.VMEM((2 * rows, 4 * WIDTH), F32),
            pltpu.VMEM((2, HEADS, rows, rows), F32),
            pltpu.SemaphoreType.DMA((4,)),
        ],
        flops=10**10,
    )
    home = exchange(payload)
    (share,) = call(sum_kernel, [((devices, CAP, 256), BF16)], [(VMEM, home)])
    shares = exchange(share)
    given_output, _ = lax.optimization_barrier((given_output, share))
    arrived_output = lax.ppermute(given_output, "dp", partners)
    narrow_grad, middle_grad, wide_grad = call(
        scatter_kernel,
        [(narrow_table.shape, F32), (middle_table.shape, F32), (wide_table.shape, F32)],
        [(VMEM, home), (VMEM, asked), (KEPT, marks)],
        flops=3 * 10**9,
    )
    output, narrow_delta, middle_delta, wide_delta = call(
        finish_kernel,
        [
            (cotangent.shape, BF16), (narrow_lift.shape, F32), (middle_lift.shape, F32), (wide_lift.shape, F32),
        ],
        [(KEPT, facts), (VMEM, kept_output), (VMEM, arrived_output), (VMEM, shares)],
    )
    return (output, narrow_grad, middle_grad, wide_grad, narrow_delta, middle_delta, wide_delta)


def solution(mesh):
    in_specs = (
        P(None, "table"),
        P(None, "table"),
        P(("dp", "table"), None, None),
        P(("dp", "table"), None),
        P(),
        P(("dp", "table")),
        P(("dp", "table"), None),
        P(("dp", "table"), None),
        P(("dp", "table"), None),
        P(),
        P(),
        P(),
        P(),
        P(),
        P(("dp", "table"), None, None),
    )
    out_specs = (
        P(("dp", "table"), None, None),
        P(("dp", "table"), None),
        P(("dp", "table"), None),
        P(("dp", "table"), None),
        P(),
        P(),
        P(),
    )
    return jax.shard_map(body, mesh=mesh, in_specs=in_specs, out_specs=out_specs, check_vma=False)
```

```python
import jax
import jax.numpy as jnp
from jax import lax
from jax.experimental import pallas as pl
from jax.experimental.pallas import tpu as pltpu
from jax.sharding import PartitionSpec as P

HEADS = 4
HEAD = 128
MAXLEN = 256
WIDTH = 512
CAP = 8
LANES = 128
OWNER_STEP = 256
LIMIT = 32

F32 = jnp.float32
BF16 = jnp.bfloat16
I32 = jnp.int32


def iota(shape, dim):
    return lax.broadcasted_iota(I32, shape, dim)


def one_hot(mask):
    return jnp.where(mask, 1.0, 0.0).astype(BF16)


def dot(a, b):
    return jnp.dot(a, b, preferred_element_type=F32)


def dot_nt(a, b):
    return lax.dot_general(a, b, (((1,), (1,)), ((), ())), preferred_element_type=F32)


def dot_tn(a, b):
    return lax.dot_general(a, b, (((0,), (0,)), ((), ())), preferred_element_type=F32)


def to_column(row):
    eye = iota((LANES, LANES), 0) == iota((LANES, LANES), 1)
    parts = []
    for start in range(0, row.shape[1], LANES):
        piece = row[:, start : start + LANES].astype(F32)
        parts.append(jnp.sum(jnp.where(eye, piece, 0.0), axis=1, keepdims=True))
    return jnp.concatenate(parts, axis=0).astype(I32)


def to_row(column):
    eye = iota((LANES, LANES), 0) == iota((LANES, LANES), 1)
    parts = []
    for start in range(0, column.shape[0], LANES):
        piece = column[start : start + LANES].astype(F32)
        parts.append(jnp.sum(jnp.where(eye, piece, 0.0), axis=0, keepdims=True))
    return jnp.concatenate(parts, axis=1).astype(I32)


def lane_sum(mask, values):
    return jnp.sum(jnp.where(mask, values, 0.0), axis=1, keepdims=True).astype(I32)


def flat_row(ref):
    return jnp.concatenate([ref[0:1, :], ref[1:2, :]], axis=1)


def request_kernel(owner_ref, item_ref, request_ref, slot_ref):
    devices = request_ref.shape[0]
    owner = jnp.concatenate([owner_ref[0], owner_ref[1]], axis=1)
    item = flat_row(item_ref)
    tokens = owner.shape[1]
    named = iota((devices, tokens), 0) == owner
    hot = one_hot(named)
    earlier = one_hot(iota((tokens, tokens), 0) < iota((tokens, tokens), 1))
    before = dot(hot, earlier)
    rank = jnp.sum(jnp.where(named, before, 0.0), axis=0, keepdims=True).astype(I32)
    place = iota((2 * CAP, tokens), 0)
    value = jnp.where(place < CAP, item >> 6, item & 63)
    table = jnp.where((place & (CAP - 1)) == rank, value, 0).astype(F32).astype(BF16)
    filled = dot_nt(hot, table).astype(I32)
    request_ref[...] = filled[:, :CAP] * 64 + filled[:, CAP:]
    slot = owner * CAP + rank
    half = tokens // 2
    slot_ref[0:1, :] = slot[:, :half]
    slot_ref[1:2, :] = slot[:, half:]


def class_kernel(owner_ref, item_ref, class_list_ref, class_ref, list_here, copied):
    copy = pltpu.make_async_copy(class_list_ref, list_here, copied)
    copy.start()
    item = to_column(flat_row(item_ref))
    owner = jnp.concatenate([owner_ref[0], owner_ref[1]], axis=1)
    line = to_column(owner) * (4096 // LANES) + (item >> 7)
    tokens = line.shape[0]
    lines = class_list_ref.shape[0]
    step = 512
    total = jnp.zeros((tokens, LANES), F32)
    copy.wait()
    for start in range(0, lines, step):
        hot = one_hot(iota((tokens, step), 1) + start == line)
        total += dot(hot, list_here[start : start + step, :].astype(F32).astype(BF16))
    kind = to_row(lane_sum(iota((tokens, LANES), 1) == (item & 127), total))
    class_ref[0:1, :] = kind[:, : tokens // 2]
    class_ref[1:2, :] = kind[:, tokens // 2 :]


def request_codes(asked_ref, marks):
    asked = asked_ref[...]
    sources = asked.shape[0]
    amount = sources * CAP
    expand = one_hot((iota((amount, sources), 0) >> 3) == iota((amount, sources), 1))
    mine = (iota((amount, CAP), 0) & (CAP - 1)) == iota((amount, CAP), 1)
    high = lane_sum(mine, dot(expand, (asked >> 7).astype(F32).astype(BF16)))
    low = lane_sum(mine, dot(expand, (asked & 127).astype(F32).astype(BF16)))
    found = dot(one_hot(iota((amount, marks.shape[0]), 1) == high), marks)
    mine = iota((amount, LANES), 1) == low
    return lane_sum(mine, found[:, LANES:]) * LANES + lane_sum(mine, found[:, :LANES])


def stage_rows_kernel(
    rank_ref, after_ref, class_list_ref, slab_ref, narrow_ref, middle_ref, wide_ref, table_ref, marks_ref,
    class_here, slab_here, copied,
):
    del after_ref
    groups = slab_here.shape[0]
    lines = narrow_ref.shape[0]
    moves = [
        (class_list_ref.at[pl.ds(pl.multiple_of(rank_ref[1] * groups, groups), groups)], class_here),
        (slab_ref, slab_here),
        (wide_ref, table_ref.at[:, 0:256]),
        (middle_ref, table_ref.at[:, 256:384]),
        (narrow_ref, table_ref.at[0:lines, 384:512]),
    ]
    copies = [pltpu.make_async_copy(there, here, copied.at[k]) for k, (there, here) in enumerate(moves)]
    for copy in copies:
        copy.start()
    table_ref[lines:, 384:] = jnp.zeros((table_ref.shape[0] - lines, LANES), BF16)
    for copy in copies:
        copy.wait()
    slab = slab_here[...]
    marks = jnp.concatenate([slab & 127, (slab >> 7) + 16 * class_here[...]], axis=1)
    marks_ref[...] = marks.astype(F32).astype(BF16)


def owner_kernel(asked_ref, marks_ref, table_ref, reply_ref):
    amount = reply_ref.shape[0]
    code = request_codes(asked_ref, marks_ref[...])
    kind = code >> 11
    slab = code & 2047
    line = jnp.where(kind == 0, slab >> 1, slab)
    lines = table_ref.shape[0]
    for start in range(0, amount, OWNER_STEP):
        rows = slice(start, start + OWNER_STEP)
        hot = one_hot(iota((OWNER_STEP, lines), 1) == line[rows])
        here = kind[rows]
        side = dot(hot, table_ref[:, 256:])
        narrow = side[:, LANES:]
        narrow = jnp.where((slab[rows] & 1) == 1, pltpu.roll(narrow, 64, 1), narrow)
        narrow = jnp.where(iota((OWNER_STEP, LANES), 1) < 64, narrow, 0.0)
        side = jnp.where(here == 1, side[:, :LANES], narrow)
        wide = dot(hot, table_ref[:, :256])
        left = jnp.where(here == 2, wide[:, :LANES], side)
        right = jnp.where(here == 2, wide[:, LANES:], 0.0)
        reply_ref[rows, :] = jnp.concatenate([left, right], axis=1).astype(BF16)


def traded_slot(rank_ref, list_ref):
    rank = rank_ref[0]
    return jnp.where((list_ref[0, rank] >> 1) != rank, 0, 1)


def stage_layer_kernel(
    rank_ref, list_ref, length_ref, after_ref, narrow_ref, middle_ref, wide_ref, joined_ref,
    facts_ref, lift_here, gating_here, values_here, copied,
):
    del after_ref
    rank = rank_ref[0]
    traded = traded_slot(rank_ref, list_ref)
    facts = [traded, list_ref[traded, rank] & 1, length_ref[0, rank], length_ref[1, rank]]
    for row, fact in enumerate(facts):
        facts_ref[row : row + 1, :] = jnp.full((1, LANES), fact, I32)
    moves = [
        (wide_ref, lift_here.at[0:256]),
        (middle_ref, lift_here.at[256:384]),
        (narrow_ref, lift_here.at[384:448]),
    ]
    for part, here in enumerate([gating_here, values_here]):
        moves.append((joined_ref.at[:, part * WIDTH : (part + 1) * WIDTH], here))
    copies = [pltpu.make_async_copy(there, here, copied.at[k]) for k, (there, here) in enumerate(moves)]
    for copy in copies:
        copy.start()
    lift_here[448:, :] = jnp.zeros((64, WIDTH), BF16)
    for copy in copies:
        copy.wait()


def mean(values):
    return jnp.sum(values, axis=1, keepdims=True) * (1.0 / WIDTH)


def normalize(values):
    centre = values - mean(values)
    scale = lax.rsqrt(mean(centre * centre) + 1e-06)
    return centre * scale, scale


def normalize_grad(grad, normed, scale):
    return scale * (grad - mean(grad) - normed * mean(grad * normed))


def sigmoid(values):
    return 0.5 * jnp.tanh(0.5 * values) + 0.5


def rounded(values):
    return values.astype(BF16).astype(F32)


def layer_kernel(
    facts_ref, slot_ref, landed_ref, class_ref, lift_here, gating_here, values_here,
    cotangent_ref, arrived_ref, joined_ref, output_weight_ref, kept_ref, given_ref, payload_ref,
    queries_here, keys_here, output_here, cotangent_here, slope_ref, curve_ref, copied,
):
    moves = [
        (joined_ref.at[:, 2 * WIDTH : 3 * WIDTH], queries_here),
        (joined_ref.at[:, 3 * WIDTH :], keys_here),
        (output_weight_ref, output_here),
        (cotangent_ref, cotangent_here),
    ]
    copies = [pltpu.make_async_copy(there, here, copied.at[k]) for k, (there, here) in enumerate(moves)]
    for copy in copies:
        copy.start()
    zero = jnp.zeros((), BF16)
    rows = kept_ref.shape[0]
    hists = slot_ref.shape[0]
    tokens = hists * rows
    devices = payload_ref.shape[0]
    amount = devices * CAP
    slot = flat_row(slot_ref)
    placing = one_hot(iota((amount, tokens), 0) == slot)
    raw = dot_tn(placing, landed_ref[...]).astype(BF16)
    kind = to_column(flat_row(class_ref))
    spread = jnp.concatenate(
        [
            jnp.where(kind == 2, raw, zero),
            jnp.where(kind == 1, raw[:, :LANES], zero),
            jnp.where(kind == 0, raw[:, :LANES], zero),
        ],
        axis=1,
    )
    widened = rounded(dot(spread, lift_here[...]))
    normed, scale = normalize(widened)
    normed_low = normed.astype(BF16)
    for copy in copies:
        copy.wait()
    joined_here = [gating_here, values_here, queries_here, keys_here]
    joined = []
    for part in range(4):
        columns = slice(part * WIDTH, (part + 1) * WIDTH)
        before = dot(normed_low, joined_here[part][...])
        gate = sigmoid(before)
        active = before * gate
        joined.append(active.astype(BF16))
        slope_ref[:, columns] = gate + active * (1.0 - gate)
    gating, values, queries, keys = joined
    gating = gating.astype(F32)
    place = iota((tokens, 1), 0)
    lengths = [facts_ref[2 + hist : 3 + hist, 0:1] for hist in range(hists)]
    traded = jnp.broadcast_to(facts_ref[0:1, 0:1], (rows, 1))
    source = jnp.broadcast_to(facts_ref[1:2, 0:1], (rows, 1))
    valid = place < jnp.where(place < rows, lengths[0], rows + lengths[1])
    across = iota((rows, rows), 1)
    causal = across <= iota((rows, rows), 0)
    weights = {}
    mixed = []
    for hist in range(hists):
        lines = slice(hist * rows, (hist + 1) * rows)
        factor = jnp.where(causal & (across < lengths[hist]), 1.0 / MAXLEN, 0.0)
        heads = []
        for head in range(HEADS):
            columns = slice(head * HEAD, (head + 1) * HEAD)
            scores = dot_nt(queries[lines, columns], keys[lines, columns])
            gate = sigmoid(scores)
            scaled = gate * factor
            active = scores * scaled
            weights[hist, head] = active.astype(BF16)
            curve_ref[hist, head] = scaled + active * (1.0 - gate)
            heads.append(dot(weights[hist, head], values[lines, columns]))
        mixed.append(jnp.concatenate(heads, axis=1))
    mixed_normed, mixed_scale = normalize(jnp.concatenate(mixed, axis=0))
    gated = (mixed_normed * gating).astype(BF16)
    result = dot(gated, output_here[...]) + widened
    output = jnp.where(valid, result, 0.0).astype(BF16)
    kept_ref[...] = jnp.where(traded == 0, output[rows:], output[:rows])
    given_ref[...] = jnp.where(traded == 0, output[:rows], output[rows:])

    came = jnp.where(source == 0, arrived_ref[0], arrived_ref[1])
    cotangent = jnp.concatenate(
        [jnp.where(traded == 0, came, cotangent_here[0]), jnp.where(traded == 0, cotangent_here[1], came)], axis=0
    )
    result_grad = jnp.where(valid, cotangent, zero)
    gated_grad = rounded(dot_nt(result_grad, output_here[...]))
    gating_grad = (gated_grad * mixed_normed).astype(BF16)
    mixed_grad = normalize_grad(gated_grad * gating, mixed_normed, mixed_scale).astype(BF16)
    grads = [[], [], []]
    for hist in range(hists):
        lines = slice(hist * rows, (hist + 1) * rows)
        heads = [[], [], []]
        for head in range(HEADS):
            columns = slice(head * HEAD, (head + 1) * HEAD)
            own = mixed_grad[lines, columns]
            weights_grad = rounded(dot_nt(own, values[lines, columns]))
            scores_grad = (weights_grad * curve_ref[hist, head]).astype(BF16)
            heads[0].append(dot_tn(weights[hist, head], own))
            heads[1].append(dot(scores_grad, keys[lines, columns]))
            heads[2].append(dot_tn(scores_grad, queries[lines, columns]))
        for part in range(3):
            grads[part].append(jnp.concatenate(heads[part], axis=1).astype(BF16))
    joined_grad = [gating_grad] + [jnp.concatenate(g, axis=0) for g in grads]
    normed_grad = jnp.zeros((tokens, WIDTH), F32)
    for part in range(4):
        columns = slice(part * WIDTH, (part + 1) * WIDTH)
        before_grad = (joined_grad[part].astype(F32) * slope_ref[:, columns]).astype(BF16)
        normed_grad += dot_nt(before_grad, joined_here[part][...])
    grad = normalize_grad(rounded(normed_grad), normed, scale) + result_grad.astype(F32)
    grad = grad.astype(BF16)
    spread_grad = dot_nt(grad, lift_here[...])
    narrow_part = jnp.where(iota((tokens, LANES), 1) < 64, spread_grad[:, 384:], 0.0)
    left = jnp.where(
        kind == 2, spread_grad[:, :LANES], jnp.where(kind == 1, spread_grad[:, 256:384], narrow_part)
    )
    right = jnp.where(kind == 2, spread_grad[:, LANES:256], 0.0)
    row_grad = jnp.concatenate([left, right], axis=1).astype(BF16)
    term = dot_tn(spread, grad).reshape(devices // 2, CAP, WIDTH)
    term = jnp.stack([term[:, :, :256], term[:, :, 256:]], axis=1).reshape(devices, CAP, 256)
    placed = dot(placing, row_grad).reshape(devices, CAP, 256)
    payload_ref[...] = jnp.concatenate([placed, term], axis=1).astype(BF16)


def sum_kernel(landed_ref, share_ref):
    total = jnp.sum(landed_ref[...].astype(F32)[:, CAP:, :], axis=0)
    share_ref[...] = jnp.broadcast_to(total[None].astype(BF16), share_ref.shape)


def scatter_kernel(landed_ref, asked_ref, marks_ref, narrow_ref, middle_ref, wide_ref):
    sources = landed_ref.shape[0]
    amount = sources * CAP
    grads = landed_ref[...].astype(F32)[:, :CAP, :].reshape(amount, 256)
    code = request_codes(asked_ref, marks_ref[...])
    kind = code >> 11
    slab = code & 2047
    line = to_row(jnp.where(kind == 0, slab >> 1, slab))
    wide = jnp.where(kind == 2, grads, 0.0).astype(BF16)
    middle = jnp.where(kind == 1, grads[:, :LANES], 0.0).astype(BF16)
    narrow = jnp.where((kind == 0) & (iota((amount, LANES), 1) < 64), grads[:, :LANES], 0.0)
    narrow = jnp.where((slab & 1) == 1, pltpu.roll(narrow, 64, 1), narrow).astype(BF16)
    step = 256
    for start in range(0, wide_ref.shape[0], step):
        hot = one_hot(iota((step, amount), 0) + start == line)
        wide_ref[start : start + step, :] = dot(hot, wide)
        middle_ref[start : start + step, :] = dot(hot, middle)
        if start < narrow_ref.shape[0]:
            narrow_ref[start : start + step, :] = dot(hot, narrow)


def finish_kernel(
    facts_ref, kept_ref, arrived_ref, shares_ref, output_ref, narrow_ref, middle_ref, wide_ref
):
    traded = jnp.broadcast_to(facts_ref[0:1, 0:1], (kept_ref.shape[0], 1))
    kept = kept_ref[...]
    arrived = arrived_ref[...]
    output_ref[0] = jnp.where(traded == 0, arrived, kept)
    output_ref[1] = jnp.where(traded == 0, kept, arrived)
    devices = shares_ref.shape[0]
    shares = shares_ref[...].astype(F32).reshape(devices // 2, 2, CAP, 256)
    for half in range(2):
        columns = slice(half * 256, (half + 1) * 256)
        whole = shares[:, half].reshape(devices // 2 * CAP, 256)
        wide_ref[:, columns] = whole[:256]
        middle_ref[:, columns] = whole[256:384]
        narrow_ref[:, columns] = whole[384:448]


SMEM = pl.BlockSpec(memory_space=pltpu.SMEM)
VMEM = pl.BlockSpec(memory_space=pltpu.VMEM)
HBM = pl.BlockSpec(memory_space=pltpu.HBM)
KEPT = pl.BlockSpec(memory_space=pltpu.VMEM)


def call(kernel, outs, args, scratch=(), flops=0, limit=LIMIT):
    arrays = []
    for space, array in args:
        if space is KEPT:
            array = pltpu.with_memory_space_constraint(array, pltpu.VMEM)
        elif space is not VMEM:
            array = pltpu.with_memory_space_constraint(array, pltpu.HBM)
        arrays.append(array)
    shapes = [
        pltpu.VMEM(out[0], out[1]) if KEPT in out[2:] else jax.ShapeDtypeStruct(out[0], out[1]) for out in outs
    ]
    moved = sum(a.size * a.dtype.itemsize for _, a in args)
    return pl.pallas_call(
        kernel,
        out_shape=shapes,
        in_specs=[space for space, _ in args],
        out_specs=[VMEM] * len(shapes),
        scratch_shapes=list(scratch),
        cost_estimate=pl.CostEstimate(flops=flops, bytes_accessed=moved, transcendentals=0),
        compiler_params=pltpu.CompilerParams(vmem_limit_bytes=int(limit * 2**20)),
    )(*arrays)


def exchange(array):
    return lax.all_to_all(array, ("dp", "table"), split_axis=0, concat_axis=0, tiled=True)


def body(
    history_lengths,
    balance_list,
    owner_device,
    owner_row,
    width_class,
    slab_index,
    narrow_table,
    middle_table,
    wide_table,
    narrow_lift,
    middle_lift,
    wide_lift,
    joined_weight,
    output_weight,
    cotangent,
):
    data_size = lax.axis_size("dp")
    table_size = lax.axis_size("table")
    devices = data_size * table_size
    rows = cotangent.shape[1]
    amount = devices * CAP
    data_rank = lax.axis_index("dp")
    self_rank = data_rank * table_size + lax.axis_index("table")
    rank = (SMEM, jnp.stack([data_rank, self_rank]).astype(I32))
    plan = (SMEM, balance_list.T)
    owner = owner_device.transpose(0, 2, 1)
    class_list = width_class.reshape(-1, LANES)
    partners = [(i, i ^ (data_size // 2)) for i in range(data_size)]

    requests, slots = call(
        request_kernel,
        [((devices, CAP), I32), (owner_row.shape, I32)],
        [(VMEM, owner), (VMEM, owner_row)],
        flops=10**8,
        limit=62,
    )
    asked = exchange(requests)
    slab_list = slab_index.reshape(-1, LANES)
    arrived_cotangent = lax.ppermute(cotangent, "dp", partners)
    table, marks = call(
        stage_rows_kernel,
        [((middle_table.shape[0], 512), BF16, KEPT), ((slab_list.shape[0], 256), BF16, KEPT)],
        [
            rank, (HBM, slots), (HBM, class_list), (HBM, slab_list),
            (HBM, narrow_table), (HBM, middle_table), (HBM, wide_table),
        ],
        scratch=[
            pltpu.VMEM(slab_list.shape, I32), pltpu.VMEM(slab_list.shape, I32), pltpu.SemaphoreType.DMA((5,)),
        ],
    )
    (replies,) = call(
        owner_kernel,
        [((amount, 256), BF16)],
        [(VMEM, asked), (KEPT, marks), (KEPT, table)],
        flops=3 * 10**9,
    )
    landed = exchange(replies)
    (kinds,) = call(
        class_kernel,
        [(owner_row.shape, I32)],
        [(VMEM, owner), (VMEM, owner_row), (HBM, class_list)],
        scratch=[pltpu.VMEM(class_list.shape, I32), pltpu.SemaphoreType.DMA],
        flops=10**9,
    )
    facts, *staged = call(
        stage_layer_kernel,
        [((8, LANES), I32, KEPT)] + [((WIDTH, WIDTH), BF16, KEPT)] * 3,
        [rank, plan, (SMEM, history_lengths.T), (HBM, slots), (HBM, narrow_lift), (HBM, middle_lift), (HBM, wide_lift), (HBM, joined_weight)],
        scratch=[pltpu.SemaphoreType.DMA((5,))],
    )
    kept_output, given_output, payload = call(
        layer_kernel,
        [((rows, WIDTH), BF16), ((rows, WIDTH), BF16), ((devices, 2 * CAP, 256), BF16)],
        [(KEPT, facts), (VMEM, slots), (VMEM, landed), (VMEM, kinds)]
        + [(KEPT, array) for array in staged]
        + [(HBM, cotangent), (VMEM, arrived_cotangent), (HBM, joined_weight), (HBM, output_weight)],
        scratch=[
            pltpu.VMEM((WIDTH, WIDTH), BF16),
            pltpu.VMEM((WIDTH, WIDTH), BF16),
            pltpu.VMEM((WIDTH, WIDTH), BF16),
            pltpu.VMEM((2, rows, WIDTH), BF16),
            pltpu.VMEM((2 * rows, 4 * WIDTH), F32),
            pltpu.VMEM((2, HEADS, rows, rows), F32),
            pltpu.SemaphoreType.DMA((4,)),
        ],
        flops=10**10,
    )
    home = exchange(payload)
    (share,) = call(sum_kernel, [((devices, CAP, 256), BF16)], [(VMEM, home)])
    shares = exchange(share)
    given_output, _ = lax.optimization_barrier((given_output, share))
    arrived_output = lax.ppermute(given_output, "dp", partners)
    narrow_grad, middle_grad, wide_grad = call(
        scatter_kernel,
        [(narrow_table.shape, F32), (middle_table.shape, F32), (wide_table.shape, F32)],
        [(VMEM, home), (VMEM, asked), (KEPT, marks)],
        flops=3 * 10**9,
    )
    output, narrow_delta, middle_delta, wide_delta = call(
        finish_kernel,
        [
            (cotangent.shape, BF16), (narrow_lift.shape, F32), (middle_lift.shape, F32), (wide_lift.shape, F32),
        ],
        [(KEPT, facts), (VMEM, kept_output), (VMEM, arrived_output), (VMEM, shares)],
    )
    return (output, narrow_grad, middle_grad, wide_grad, narrow_delta, middle_delta, wide_delta)


def solution(mesh):
    in_specs = (
        P(None, "table"),
        P(None, "table"),
        P(("dp", "table"), None, None),
        P(("dp", "table"), None),
        P(),
        P(("dp", "table")),
        P(("dp", "table"), None),
        P(("dp", "table"), None),
        P(("dp", "table"), None),
        P(),
        P(),
        P(),
        P(),
        P(),
        P(("dp", "table"), None, None),
    )
    out_specs = (
        P(("dp", "table"), None, None),
        P(("dp", "table"), None),
        P(("dp", "table"), None),
        P(("dp", "table"), None),
        P(),
        P(),
        P(),
    )
    return jax.shard_map(body, mesh=mesh, in_specs=in_specs, out_specs=out_specs, check_vma=False)
```
